256 devices in a mesh: dp: 8 (over y, x_hi), ctx: 32 (over x_lo, z, core).
Axes of the slice: x: 4 (x_hi: 2, x_lo: 2; x = x_hi * 2 + x_lo), y: 4, z: 8, core: 2. Of those that a mesh axis runs over, the one named last changes fastest.
Arguments:
- lengths: int32 [8], replicated, may hold values from 1024 to 4096, as said below
- query_states: bfloat16 [8, 4096, 512], P('dp', 'ctx'), may hold values from -60 to 60
- key_states: bfloat16 [8, 4096, 512], P('dp', 'ctx'), may hold values from -5.6 to 5.6
- value_states: bfloat16 [8, 4096, 512], P('dp', 'ctx'), may hold values from -24 to 24
- grad_output: bfloat16 [8, 4096, 512], P('dp', 'ctx'), may hold values from -6 to 6
- conv_kernel: float32 [31, 512], replicated, may hold values from -1 to 1
Outputs:
- mixed_out: bfloat16 [8, 4096, 512], P('dp', 'ctx')
- query_grad: bfloat16 [8, 4096, 512], P('dp', 'ctx')
- key_grad: bfloat16 [8, 4096, 512], P('dp', 'ctx')
- value_grad: bfloat16 [8, 4096, 512], P('dp', 'ctx')
- kernel_grad: float32 [31, 512], replicated
The draws below stay inside these ranges and needn't reach their ends.
Inputs may be any that keep to these rules, and one draw needn't show every extreme that they name: `lengths`: one recording has all 4096 frames live.
All inputs are finite; a program needn't handle non-finite values.
Results may differ from the reference program's by a relative error of at most 0.04.
Values may be sent and summed in bfloat16 or wider, within the bound.
A program may use at most 128 MiB of HBM per device.

```python
import math
import jax
import jax.numpy as jnp
from jax import lax

HEADS = 8
HEAD_DIM = 64
KERNEL = 31
WIDTH = 512
SEQ = 4096
RECS = 8


def key_parts(key):
    shape = (RECS, SEQ, HEADS * HEAD_DIM)
    normal_part = jax.random.normal(jax.random.fold_in(key, 11), shape, jnp.float32)
    return normal_part


def draw_lengths(key, part):
    key = jax.random.fold_in(key, 2)
    values = jax.random.randint(jax.random.fold_in(key, 1), (RECS,), SEQ // 4, SEQ + 1, dtype=jnp.int32)
    fullest = jax.random.randint(jax.random.fold_in(key, 2), (), 0, RECS, dtype=jnp.int32)
    return jnp.where(jnp.arange(RECS, dtype=jnp.int32) == fullest, SEQ, values).astype(jnp.int32)


def draw_key_states(key, part):
    normal_part = key_parts(key)
    return (1.4 * jnp.clip(normal_part, -4.0, 4.0)).astype(jnp.bfloat16)


def draw_query_states(key, part):
    key = jax.random.fold_in(key, 4)
    drawn = 1.4 * jnp.clip(jax.random.normal(key, (RECS, SEQ, HEADS * HEAD_DIM), jnp.float32), -4.0, 4.0)
    return drawn.astype(jnp.bfloat16)


def block_scale(own_key, dims, shards, least, top_value):
    factor_of, own = 1.0, jax.random.fold_in(own_key, 6)
    for axis_at, shards_of in shards:
        steps = jnp.exp(jax.random.uniform(jax.random.fold_in(own, axis_at), (shards_of,), jnp.float32, least / len(shards), top_value / len(shards)))
        factor_of = factor_of * jnp.repeat(steps, dims[axis_at] // shards_of).reshape([-1 if axis == axis_at else 1 for axis in range(len(dims))])
    return factor_of


def centred(stream_key, extent, width, bound, cuts=(), kind=jnp.bfloat16):
    entries = jax.random.normal(stream_key, extent, jnp.float32) * width
    if len(cuts) > 0:
        entries = block_scale(stream_key, extent, cuts, -0.22, 0.18) * entries
    return jnp.clip(entries, min=-bound, max=bound).astype(kind)


def setup_inputs(seed: int = 0) -> dict:
    arg_keys = jax.random.split(jax.random.key(seed), 7)
    lengths = draw_lengths(jax.random.fold_in(arg_keys[6], 71), 0)
    query_states = draw_query_states(jax.random.fold_in(arg_keys[6], 71), 0)
    key_states = draw_key_states(jax.random.fold_in(arg_keys[6], 71), 0)
    value_states = centred(arg_keys[3], (RECS, SEQ, WIDTH), 4.0, 24.0, ((0, 8), (1, 32)))
    grad_output = centred(arg_keys[4], (RECS, SEQ, WIDTH), 1.0, 6.0, ((0, 8), (1, 32)))
    conv_kernel = centred(arg_keys[5], (KERNEL, WIDTH), KERNEL ** -0.5, 1.0, (), jnp.float32)
    return dict(lengths=lengths, query_states=query_states, key_states=key_states, value_states=value_states, grad_output=grad_output, conv_kernel=conv_kernel)


MASK_FILL = -1e30


def time_conv(signal, kernel):
    half_width = (kernel.shape[0] - 1) // 2
    count = signal.shape[0]
    padded = jnp.pad(signal, ((half_width, half_width), (0, 0)))
    result = jnp.zeros(signal.shape, jnp.float32)
    for tap in range(kernel.shape[0]):
        result = result + kernel[tap] * padded[tap:tap + count]
    return result, padded


def time_conv_back(signal, kernel):
    half_width = (kernel.shape[0] - 1) // 2
    count = signal.shape[0]
    padded = jnp.pad(signal, ((half_width, half_width), (0, 0)))
    result = jnp.zeros(signal.shape, jnp.float32)
    for tap in range(kernel.shape[0]):
        begin = 2 * half_width - tap
        result = result + kernel[tap] * padded[begin:begin + count]
    return result, padded


def one_record(query, keys, values, cotangent, length, kernel):
    seq_rows = query.shape[0]
    feature_width = query.shape[1]
    score_scale = HEAD_DIM ** -0.5
    block_rows = math.gcd(seq_rows, 512)
    blocks = seq_rows // block_rows
    live_rows = jnp.arange(seq_rows, dtype=jnp.int32) < length
    live_column = live_rows.astype(jnp.float32)[:, None]
    key_heads = keys.astype(jnp.float32).reshape(seq_rows, HEADS, HEAD_DIM)
    value_heads = values.astype(jnp.float32).reshape(seq_rows, HEADS, HEAD_DIM)
    query_blocks = query.astype(jnp.float32).reshape(blocks, block_rows, HEADS, HEAD_DIM)

    def forward_block(query_block):
        scores = jnp.einsum("qhd,khd->hqk", query_block, key_heads) * score_scale
        scores = jnp.where(live_rows[None, None, :], scores, MASK_FILL)
        row_max = jnp.max(scores, axis=2)
        weights = jnp.where(live_rows[None, None, :], jnp.exp(scores - row_max[:, :, None]), 0.0)
        denominator = jnp.sum(weights, axis=2)
        rounded = weights.astype(jnp.bfloat16).astype(jnp.float32)
        context = jnp.einsum("hqk,khd->qhd", rounded, value_heads)
        context = context / denominator.T[:, :, None]
        return context.reshape(block_rows, feature_width).astype(jnp.bfloat16), row_max + jnp.log(denominator)

    attention, lse_blocks = lax.map(forward_block, query_blocks)
    attention = attention.reshape(seq_rows, feature_width)
    attention_live = (attention.astype(jnp.float32) * live_column).astype(jnp.bfloat16).astype(jnp.float32)
    conv_out, attention_padded = time_conv(attention_live, kernel)
    mixed = ((attention_live + conv_out) * live_column).astype(jnp.bfloat16)
    grad_live = (cotangent.astype(jnp.float32) * live_column).astype(jnp.bfloat16).astype(jnp.float32)
    conv_back, unused_padded = time_conv_back(grad_live, kernel)
    out_grad = ((grad_live + conv_back) * live_column).astype(jnp.bfloat16)
    kernel_terms = jnp.stack([jnp.sum(grad_live * attention_padded[tap:tap + seq_rows], axis=0) for tap in range(kernel.shape[0])])
    out_grad_f = out_grad.astype(jnp.float32)
    delta = jnp.sum((out_grad_f * attention.astype(jnp.float32)).reshape(seq_rows, HEADS, HEAD_DIM), axis=2)
    delta_blocks = delta.reshape(blocks, block_rows, HEADS).transpose(0, 2, 1)
    grad_blocks = out_grad_f.reshape(blocks, block_rows, HEADS, HEAD_DIM)

    def backward_block(running, inputs):
        query_block, grad_block, lse_block, delta_block = inputs
        scores = jnp.einsum("qhd,khd->hqk", query_block, key_heads) * score_scale
        probs = jnp.where(live_rows[None, None, :], jnp.exp(scores - lse_block[:, :, None]), 0.0)
        prob_grad = jnp.einsum("qhd,khd->hqk", grad_block, value_heads)
        score_grad = (probs * (prob_grad - delta_block[:, :, None])).astype(jnp.bfloat16).astype(jnp.float32)
        query_part = jnp.einsum("hqk,khd->qhd", score_grad, key_heads) * score_scale
        key_sum = running[0] + jnp.einsum("hqk,qhd->khd", score_grad, query_block)
        rounded = probs.astype(jnp.bfloat16).astype(jnp.float32)
        value_sum = running[1] + jnp.einsum("hqk,qhd->khd", rounded, grad_block)
        return (key_sum, value_sum), query_part.reshape(block_rows, feature_width).astype(jnp.bfloat16)

    zero_heads = jnp.zeros((seq_rows, HEADS, HEAD_DIM), jnp.float32)
    sums, query_grad = lax.scan(backward_block, (zero_heads, zero_heads), (query_blocks, grad_blocks, lse_blocks, delta_blocks))
    key_grad = (score_scale * sums[0]).reshape(seq_rows, feature_width).astype(jnp.bfloat16)
    value_grad = sums[1].reshape(seq_rows, feature_width).astype(jnp.bfloat16)
    return mixed, query_grad.reshape(seq_rows, feature_width), key_grad, value_grad, kernel_terms


def reference(lengths, query_states, key_states, value_states, grad_output, conv_kernel):
    mixed_list = []
    query_list = []
    key_list = []
    value_list = []
    kernel_grad = jnp.zeros(conv_kernel.shape, jnp.float32)
    for record in range(lengths.shape[0]):
        results = one_record(query_states[record], key_states[record], value_states[record], grad_output[record], lengths[record], conv_kernel)
        mixed_list.append(results[0])
        query_list.append(results[1])
        key_list.append(results[2])
        value_list.append(results[3])
        kernel_grad = kernel_grad + results[4]
    return (jnp.stack(mixed_list), jnp.stack(query_list), jnp.stack(key_list), jnp.stack(value_list), kernel_grad)
```

```python
import functools

import jax
import jax.numpy as jnp
from jax import lax
from jax.experimental import pallas as pl
from jax.experimental.pallas import tpu as pltpu
from jax.sharding import PartitionSpec as P

MESH = pl.DeviceIdType.MESH
D = 64
R = 128
FILL = -1e30
F32 = jnp.float32
BF16 = jnp.bfloat16

NN = (((1,), (0,)), ((), ()))
NT = (((1,), (1,)), ((), ()))


def dot(a, b, dims=NN):
    return lax.dot_general(a, b, dims, preferred_element_type=F32)


def kernel(
    Z, NDP, CK,
    len_ref, q_ref, k_ref, v_ref, g_ref, ck_ref,
    mix_out, dq_out, dk_out, dv_out, kg_out,
    snd_kv, snd_q, snd_g, kvt, kvn, kaug, qt, qaug, gseq, oseq, dot_t, gfc,
    kb, kga, kgt, kg_grp, kg_dp, kg_z, kg_s1, kg_s2,
    w_all, m_all, m_run, l_run, acc, dq_acc, mix_s, dq_s, part, gred, kv_s, rcv_m, rcv_q, rcv_kv,
    s_kv, r_kv, s_q, r_q, s_g, r_g, s_grp, r_grp, s_h, r_h,
    s_kg, r_kg, s_m, r_m, s_dq, r_dq, s_p, r_p, s_o, r_o,
):
    NQ = R * Z
    T = ck_ref.shape[0]
    HALF = (T - 1) // 2
    me = lax.axis_index("ctx")
    dp = lax.axis_index("dp")
    x = me // (2 * Z)
    z = (me // 2) % Z
    c = me % 2
    gm = 2 * x + c
    length = len_ref[dp]

    def zpeer(p):
        return (dp, x * 2 * Z + 2 * p + c)

    def gpeer(g):
        return (dp, (g // 2) * 2 * Z + 2 * z + g % 2)

    def rcopy(src, dst, ssem, rsem, dev):
        return pltpu.make_async_remote_copy(
            src_ref=src, dst_ref=dst, send_sem=ssem, recv_sem=rsem, device_id=dev, device_id_type=MESH
        )

    zorder = []
    for i in range(1, Z // 2 + 1):
        zorder.append(i)
        if Z - i != i:
            zorder.append(Z - i)

    zero_blk = jnp.zeros((D, R), BF16)
    for s in (gseq, oseq):
        s[0, 0] = zero_blk
        s[Z, 1] = zero_blk

    barrier = pltpu.get_barrier_semaphore()
    for i in range(1, Z):
        pl.semaphore_signal(barrier, inc=1, device_id=zpeer((z + i) % Z), device_id_type=MESH)
    for i in range(1, 4):
        pl.semaphore_signal(barrier, inc=1, device_id=gpeer((gm + i) % 4), device_id_type=MESH)
    for i in range(1, NDP):
        pl.semaphore_signal(barrier, inc=1, device_id=((dp + i) % NDP, me), device_id_type=MESH)

    my_frames = me * R + lax.broadcasted_iota(jnp.int32, (1, R), 1)
    my_live = (my_frames < length).astype(F32)
    turned = lambda ref: ref[...].astype(F32).T
    snd_q[...] = turned(q_ref).astype(BF16).reshape(Z, D, R)
    snd_kv[:, 0:D, :] = turned(k_ref).astype(BF16).reshape(Z, D, R)
    snd_kv[:, D : 2 * D, :] = turned(v_ref).astype(BF16).reshape(Z, D, R)
    snd_g[...] = (turned(g_ref) * my_live).astype(BF16).reshape(Z, D, R)

    pl.semaphore_wait(barrier, (Z - 1) + 3 + (NDP - 1))

    def cols(j):
        return pl.ds(pl.multiple_of(j * R, R), R)

    def seq_at(ref, p):
        return ref.at[p // 2, p % 2]

    sends = []
    for i in zorder:
        p = (z + i) % Z
        cp = rcopy(snd_kv.at[p], kvt.at[gm, :, cols(z)], s_kv.at[i], r_kv.at[z], zpeer(p))
        cp.start()
        sends.append(cp)
    for i in zorder:
        p = (z + i) % Z
        cp = rcopy(snd_q.at[p], qt.at[:, cols(z)], s_q.at[i], r_q.at[z], zpeer(p))
        cp.start()
        sends.append(cp)
    for i in zorder:
        p = (z + i) % Z
        cp = rcopy(snd_g.at[p], seq_at(gseq, 1 + 2 * z + c), s_g.at[i], r_g.at[z], zpeer(p))
        cp.start()
        sends.append(cp)
    kvt[gm, :, cols(z)] = snd_kv[z]
    qt[:, cols(z)] = snd_q[z]
    gseq[(1 + 2 * z + c) // 2, (1 + 2 * z + c) % 2] = snd_g[z]

    kgt[...] = jnp.zeros_like(kgt)
    kgt[0:T, :] = ck_ref[...]
    for b in range(Z * D // R):
        kg_s1[b * R : (b + 1) * R, :] = kgt[:, b * R : (b + 1) * R].T
    my_taps = kg_s1[pl.ds(pl.multiple_of(z * D, D), D), :]
    for t in range(T):
        kb[t] = jnp.broadcast_to(my_taps[:, t : t + 1], (D, R))

    for i in zorder:
        p = (z + i) % Z
        rcopy(snd_kv.at[p], kvt.at[gm, :, cols(p)], s_kv.at[i], r_kv.at[p], zpeer(p)).wait_recv()
    for i in range(1, 4):
        cp = rcopy(kvt.at[gm], kvt.at[gm], s_grp.at[i], r_grp.at[gm], gpeer((gm + i) % 4))
        cp.start()
        sends.append(cp)
    for i in zorder:
        p = (z + i) % Z
        rcopy(snd_q.at[p], qt.at[:, cols(p)], s_q.at[i], r_q.at[p], zpeer(p)).wait_recv()
    for i in zorder:
        p = (z + i) % Z
        rcopy(snd_g.at[p], seq_at(gseq, 1 + 2 * p + c), s_g.at[i], r_g.at[p], zpeer(p)).wait_recv()

    def halo(seq, n):
        mine = seq.at[pl.ds(c, Z), 1 - c]
        cp = rcopy(mine, mine, s_h.at[n], r_h.at[n], gpeer(gm + 1 - 2 * c))
        cp.start()

        @pl.when(x != c)
        def _():
            rcopy(
                seq.at[c * Z, 1 - c], seq.at[(1 - c) * Z, 1 - c],
                s_h.at[n + 1], r_h.at[n + 1], gpeer(3 - gm),
            ).start()

    def halo_wait(seq, n):
        mine = seq.at[pl.ds(c, Z), 1 - c]
        other = seq.at[pl.ds(1 - c, Z), c]
        cp = rcopy(mine, other, s_h.at[n], r_h.at[n], gpeer(gm + 1 - 2 * c))
        cp.wait_send()
        cp.wait_recv()

        @pl.when(x != c)
        def _():
            cp2 = rcopy(
                seq.at[c * Z, 1 - c], seq.at[c * Z, c],
                s_h.at[n + 1], r_h.at[n + 1], gpeer(3 - gm),
            )
            cp2.wait_send()
            cp2.wait_recv()

    halo(gseq, 0)
    qaug[0:D, :] = (qt[...].astype(F32) * (D ** -0.5)).astype(BF16)
    row = lax.broadcasted_iota(jnp.int32, (D, NQ), 0)
    qaug[D : 2 * D, :] = jnp.where(row == 0, 1.0, 0.0).astype(BF16)
    halo_wait(gseq, 0)

    lane = lax.broadcasted_iota(jnp.int32, (1, R), 1)

    def live_of(j):
        return ((x * 2 * Z + 2 * j + c) * R + lane < length).astype(F32)

    def window(seq, j):
        p = 1 + 2 * j + c
        parts = [seq[(p + d) // 2, (p + d) % 2].astype(F32) for d in (-1, 0, 1)]
        return jnp.concatenate(parts, axis=1), parts[1]

    def shifted(wide, s):
        if s == 0:
            return wide[:, R : 2 * R]
        return pltpu.roll(wide, (3 * R - s) % (3 * R), 1)[:, R : 2 * R]

    def grad_block(j, carry):
        wide, mid = window(gseq, j)
        total = mid
        for t in range(T):
            total = total + kb[t] * shifted(wide, HALF - t)
        dot_t[:, cols(j)] = (total * live_of(j)).astype(BF16)
        return carry

    lax.fori_loop(0, Z, grad_block, 0)

    for i in range(1, 4):
        g = (gm + i) % 4
        rcopy(kvt.at[g], kvt.at[g], s_grp.at[i], r_grp.at[g], gpeer(g)).wait_recv()

    lane_full = lax.broadcasted_iota(jnp.int32, (R, R), 1)
    sub_full = lax.broadcasted_iota(jnp.int32, (R, R), 0)

    def turn_block(n, carry):
        g = n // Z
        j = n % Z
        blk = kvt[g, :, cols(j)].astype(F32).T
        at = pl.ds(pl.multiple_of(n * R, R), R)
        kvn[at, :] = blk.astype(BF16)
        frame = ((g // 2) * 2 * Z + 2 * j + g % 2) * R + sub_full
        fill = jnp.where((lane_full == D) & (frame >= length), FILL, 0.0)
        kaug[at, :] = jnp.where(lane_full < D, blk, fill).astype(BF16)
        return carry

    lax.fori_loop(0, 4 * Z, turn_block, 0)

    m_run[...] = jnp.full(m_run.shape, FILL, F32)
    l_run[...] = jnp.zeros_like(l_run)
    acc[...] = jnp.zeros_like(acc)
    per_g = NQ // CK

    def forward(n, carry):
        at = pl.ds(pl.multiple_of(n * CK, CK), CK)
        s = dot(kaug[at, :], qaug[...])
        m_old = m_run[0:1, :]
        m_new = jnp.maximum(m_old, jnp.max(s, axis=0, keepdims=True))
        w = jnp.exp(s - m_new)
        alpha = jnp.exp(m_old - m_new)
        l_run[0:1, :] = l_run[0:1, :] * alpha + jnp.sum(w, axis=0, keepdims=True)
        wb = w.astype(BF16)
        w_all[at, :] = wb
        lanes = pl.ds(pl.multiple_of((n % per_g) * CK, CK), CK)
        acc[...] = acc[...] * alpha + dot(kvt[n // per_g, D : 2 * D, lanes], wb)
        m_run[0:1, :] = m_new
        m_all[n, 0:1, :] = m_new
        return carry

    lax.fori_loop(0, 4 * per_g, forward, 0)

    inv = 1.0 / l_run[0:1, :]
    l_run[0:1, :] = inv
    att = (acc[...] * inv).astype(BF16)
    for j in range(Z):
        blk = (att[:, j * R : (j + 1) * R].astype(F32) * live_of(j)).astype(BF16)
        oseq[(1 + 2 * j + c) // 2, (1 + 2 * j + c) % 2] = blk
    delta = jnp.sum(dot_t[...].astype(F32) * att.astype(F32), axis=0, keepdims=True)
    m_fin = m_run[0:1, :]
    halo(oseq, 2)
    kga[...] = jnp.zeros_like(kga)
    halo_wait(oseq, 2)

    def out_block(j, carry):
        wide, mid = window(oseq, j)
        p = 1 + 2 * j + c
        grad = gseq[p // 2, p % 2].astype(F32)
        total = mid
        for t in range(T):
            seg = shifted(wide, t - HALF)
            total = total + kb[t] * seg
            kga[t] = kga[t] + grad * seg
        mix_s[j] = (total * live_of(j)).astype(BF16)
        return carry

    lax.fori_loop(0, Z, out_block, 0)

    for i in zorder:
        p = (z + i) % Z
        cp = rcopy(mix_s.at[p], rcv_m.at[z], s_m.at[i], r_m.at[z], zpeer(p))
        cp.start()
        sends.append(cp)
    rcv_m[z] = mix_s[z]

    lane_d = lax.broadcasted_iota(jnp.int32, (D, R), 1)
    red = jnp.zeros((D, R), F32)
    for t in range(T):
        red = jnp.where(lane_d == t, jnp.sum(kga[t], axis=1, keepdims=True), red)
    kg_grp[gm] = jnp.concatenate([red, jnp.zeros((R - D, R), F32)], axis=0).T[0:32, :]
    for i in range(1, 4):
        cp = rcopy(kg_grp.at[gm], kg_grp.at[gm], s_kg.at[i], r_kg.at[gm], gpeer((gm + i) % 4))
        cp.start()
        sends.append(cp)

    dq_acc[...] = jnp.zeros_like(dq_acc)
    gfc[0:D, :] = jnp.zeros((D, NQ), BF16)
    m_run[1:2, :] = delta

    def backward(n, carry):
        at = pl.ds(pl.multiple_of(n * CK, CK), CK)
        lanes = pl.ds(pl.multiple_of((n % per_g) * CK, CK), CK)
        g = n // per_g
        f = jnp.exp(m_all[n, 0:1, :] - m_run[0:1, :]) * l_run[0:1, :]
        gf = (dot_t[...].astype(F32) * f).astype(BF16)
        gfc[D : 2 * D, :] = gf
        dp_t = dot(kvn[at, :], gfc[...])
        wb = w_all[at, :]
        ds = (wb.astype(F32) * (dp_t - m_run[1:2, :] * f)).astype(BF16)
        dq_acc[...] = dq_acc[...] + dot(kvt[g, 0:D, lanes], ds)
        part[g, 0:D, lanes] = (dot(qt[...], ds, NT) * (D ** -0.5)).astype(BF16)
        part[g, D : 2 * D, lanes] = dot(gf, wb, NT).astype(BF16)
        return carry

    lax.fori_loop(0, 4 * per_g, backward, 0)

    for i in range(1, 4):
        g = (gm + i) % 4
        cp = rcopy(part.at[g], gred.at[gm], s_p.at[i], r_p.at[gm], gpeer(g))
        cp.start()
        sends.append(cp)

    for j in range(Z):
        dq_s[j] = (dq_acc[:, j * R : (j + 1) * R] * (D ** -0.5)).astype(BF16)
    for i in zorder:
        p = (z + i) % Z
        cp = rcopy(dq_s.at[p], rcv_q.at[z], s_dq.at[i], r_dq.at[z], zpeer(p))
        cp.start()
        sends.append(cp)
    rcv_q[z] = dq_s[z]

    for i in range(1, 4):
        g = (gm + i) % 4
        rcopy(kg_grp.at[g], kg_grp.at[g], s_kg.at[i], r_kg.at[g], gpeer(g)).wait_recv()
    kg_dp[dp] = (kg_grp[0] + kg_grp[1]) + (kg_grp[2] + kg_grp[3])
    for i in range(1, NDP):
        cp = rcopy(kg_dp.at[dp], kg_dp.at[dp], s_kg.at[4 + i], r_kg.at[4 + dp], ((dp + i) % NDP, me))
        cp.start()
        sends.append(cp)

    gred[gm] = part[gm]
    for i in range(1, 4):
        g = (gm + i) % 4
        rcopy(part.at[g], gred.at[g], s_p.at[i], r_p.at[g], gpeer(g)).wait_recv()
    for j in range(Z):
        at = slice(j * R, (j + 1) * R)
        total = (gred[0, :, at].astype(F32) + gred[1, :, at].astype(F32)) + (
            gred[2, :, at].astype(F32) + gred[3, :, at].astype(F32)
        )
        kv_s[j] = total.astype(BF16)
    for i in zorder:
        p = (z + i) % Z
        cp = rcopy(kv_s.at[p], rcv_kv.at[z], s_o.at[i], r_o.at[z], zpeer(p))
        cp.start()
        sends.append(cp)
    rcv_kv[z] = kv_s[z]

    for i in range(1, NDP):
        p = (dp + i) % NDP
        rcopy(kg_dp.at[p], kg_dp.at[p], s_kg.at[4 + i], r_kg.at[4 + p], (p, me)).wait_recv()
    total = kg_dp[0]
    for i in range(1, NDP):
        total = total + kg_dp[i]
    kg_z[z] = total
    for i in zorder:
        p = (z + i) % Z
        cp = rcopy(kg_z.at[z], kg_z.at[z], s_kg.at[4 + NDP + i], r_kg.at[4 + NDP + z], zpeer(p))
        cp.start()
        sends.append(cp)

    def turned_out(a):
        return a.astype(F32).reshape(Z * D, R).T.astype(BF16)

    for i in zorder:
        p = (z + i) % Z
        rcopy(mix_s.at[p], rcv_m.at[p], s_m.at[i], r_m.at[p], zpeer(p)).wait_recv()
    mix_out[...] = turned_out(rcv_m[...])
    for i in zorder:
        p = (z + i) % Z
        rcopy(dq_s.at[p], rcv_q.at[p], s_dq.at[i], r_dq.at[p], zpeer(p)).wait_recv()
    dq_out[...] = turned_out(rcv_q[...])
    for i in zorder:
        p = (z + i) % Z
        rcopy(kv_s.at[p], rcv_kv.at[p], s_o.at[i], r_o.at[p], zpeer(p)).wait_recv()
    dk_out[...] = turned_out(rcv_kv[:, 0:D, :])
    dv_out[...] = turned_out(rcv_kv[:, D : 2 * D, :])
    for i in zorder:
        p = (z + i) % Z
        rcopy(kg_z.at[p], kg_z.at[p], s_kg.at[4 + NDP + i], r_kg.at[4 + NDP + p], zpeer(p)).wait_recv()
    for h in range(0, Z, 2):
        both = jnp.concatenate([kg_z[h][0:T, 0:D], kg_z[h + 1][0:T, 0:D]], axis=1)
        kg_out[:, h * D : (h + 2) * D] = both

    for cp in sends:
        cp.wait_send()


def per_device(Z, NDP, lengths, q, k, v, g, taps):
    W = Z * D
    NQ = R * Z
    NK = 4 * NQ
    T = taps.shape[0]
    CK = min(512, NQ)
    NC = NK // CK
    vm = pltpu.VMEM
    dma = pltpu.SemaphoreType.DMA
    scratch = [
        vm((Z, 2 * D, R), BF16), vm((Z, D, R), BF16), vm((Z, D, R), BF16),
        vm((4, 2 * D, NQ), BF16), vm((NK, 2 * D), BF16), vm((NK, 2 * D), BF16),
        vm((D, NQ), BF16), vm((2 * D, NQ), BF16),
        vm((Z + 1, 2, D, R), BF16), vm((Z + 1, 2, D, R), BF16),
        vm((D, NQ), BF16), vm((2 * D, NQ), BF16),
        vm((T, D, R), F32), vm((T, D, R), F32), vm((R, W), F32),
        vm((4, 32, R), F32), vm((NDP, 32, R), F32), vm((Z, 32, R), F32), vm((W, R), F32), vm((8, R), F32),
        vm((NK, NQ), BF16), vm((NC, 8, NQ), F32), vm((8, NQ), F32), vm((8, NQ), F32),
        vm((D, NQ), F32), vm((D, NQ), F32),
        vm((Z, D, R), BF16), vm((Z, D, R), BF16),
        vm((4, 2 * D, NQ), BF16), vm((4, 2 * D, NQ), BF16), vm((Z, 2 * D, R), BF16),
        vm((Z, D, R), BF16), vm((Z, D, R), BF16), vm((Z, 2 * D, R), BF16),
        dma((Z,)), dma((Z,)), dma((Z,)), dma((Z,)), dma((Z,)), dma((Z,)),
        dma((4,)), dma((4,)), dma((4,)), dma((4,)),
        dma((4 + NDP + Z,)), dma((4 + NDP + Z,)), dma((Z,)), dma((Z,)), dma((Z,)), dma((Z,)),
        dma((4,)), dma((4,)), dma((Z,)), dma((Z,)),
    ]
    vspec = pl.BlockSpec(memory_space=pltpu.VMEM)
    outs = pl.pallas_call(
        functools.partial(kernel, Z, NDP, CK),
        out_shape=(
            jax.ShapeDtypeStruct((R, W), BF16), jax.ShapeDtypeStruct((R, W), BF16),
            jax.ShapeDtypeStruct((R, W), BF16), jax.ShapeDtypeStruct((R, W), BF16),
            jax.ShapeDtypeStruct((T, W), F32),
        ),
        in_specs=[pl.BlockSpec(memory_space=pltpu.SMEM)] + [vspec] * 5,
        out_specs=(vspec,) * 5,
        scratch_shapes=scratch,
        compiler_params=pltpu.CompilerParams(
            collective_id=0, has_side_effects=True, vmem_limit_bytes=56 * 1024 * 1024
        ),
        cost_estimate=pl.CostEstimate(
            flops=12 * NQ * NK * D, bytes_accessed=9 * R * W * 2, transcendentals=NQ * NK
        ),
    )(lengths, q[0], k[0], v[0], g[0], taps)
    return outs[0][None], outs[1][None], outs[2][None], outs[3][None], outs[4]


def solution(mesh):
    Z = mesh.shape["ctx"] // 4
    NDP = mesh.shape["dp"]
    split = P("dp", "ctx", None)
    return jax.shard_map(
        functools.partial(per_device, Z, NDP),
        mesh=mesh,
        in_specs=(P(), split, split, split, split, P()),
        out_specs=(split, split, split, split, P()),
        check_vma=False,
    )
```

```python
import functools

import jax
import jax.numpy as jnp
from jax import lax
from jax.experimental import pallas as pl
from jax.experimental.pallas import tpu as pltpu
from jax.sharding import PartitionSpec as P

MESH = pl.DeviceIdType.MESH
D = 64
R = 128
FILL = -1e30
F32 = jnp.float32
BF16 = jnp.bfloat16

NN = (((1,), (0,)), ((), ()))
NT = (((1,), (1,)), ((), ()))


def dot(a, b, dims=NN):
    return lax.dot_general(a, b, dims, preferred_element_type=F32)


def kernel(
    Z, NDP,
    len_ref, q_hbm, k_hbm, v_hbm, g_hbm, ck_hbm,
    land, kg_land,
    q_in, k_in, v_in, g_in, ck_in,
    snd_kv, snd_q, snd_g, kvt, kvn, kaug, qt, qaug, gseq, oseq, dot_t, gfc,
    kb, kga, kgt, kg_grp, kg_dp, kg_s, kg_s1,
    w_all, m_all, m_run, l_run, acc, dq_acc, mix_s, dq_s, part, gred, kv_s,
    s_in, s_kv, r_kv, s_q, r_q, s_g, r_g, s_grp, r_grp, s_h, r_h,
    s_kg, r_kg, s_m, r_m, s_dq, r_dq, s_p, r_p, s_o, r_o, s_loc,
):
    NQ = R * Z
    CK = 4 * R
    T = ck_in.shape[0]
    HALF = (T - 1) // 2
    me = lax.axis_index("ctx")
    dp = lax.axis_index("dp")
    x = me // (2 * Z)
    z = (me // 2) % Z
    c = me % 2
    gm = 2 * x + c
    length = len_ref[dp]

    def zpeer(p):
        return (dp, x * 2 * Z + 2 * p + c)

    def gpeer(g):
        return (dp, (g // 2) * 2 * Z + 2 * z + g % 2)

    def rcopy(src, dst, ssem, rsem, dev):
        return pltpu.make_async_remote_copy(
            src_ref=src, dst_ref=dst, send_sem=ssem, recv_sem=rsem, device_id=dev, device_id_type=MESH
        )

    offs = [0]
    for i in range(1, Z // 2 + 1):
        offs.append(i)
        if Z - i != i:
            offs.append(Z - i)
    zorder = offs[1:]
    slot_of = {o: n for n, o in enumerate(offs)}

    def off_of(n):
        odd = n % 2
        return odd * ((n + 1) // 2) + (1 - odd) * ((Z - n // 2) % Z)

    zero_blk = jnp.zeros((D, R), BF16)
    for s in (gseq, oseq):
        s[0, 0] = zero_blk
        s[Z, 1] = zero_blk

    barrier = pltpu.get_barrier_semaphore()
    for i in range(1, Z):
        pl.semaphore_signal(barrier, inc=1, device_id=zpeer((z + i) % Z), device_id_type=MESH)
    for i in range(1, 4):
        pl.semaphore_signal(barrier, inc=1, device_id=gpeer((gm + i) % 4), device_id_type=MESH)
    for i in range(1, NDP):
        pl.semaphore_signal(barrier, inc=1, device_id=((dp + i) % NDP, me), device_id_type=MESH)

    loads = []
    for n, (a, b) in enumerate(((g_hbm, g_in), (q_hbm, q_in), (k_hbm, k_in), (v_hbm, v_in), (ck_hbm, ck_in))):
        cp = pltpu.make_async_copy(a, b, s_in.at[n])
        cp.start()
        loads.append(cp)

    my_frames = me * R + lax.broadcasted_iota(jnp.int32, (1, R), 1)
    my_live = (my_frames < length).astype(F32)
    turned = lambda ref: ref[...].astype(F32).T
    loads[0].wait()
    snd_g[...] = (turned(g_in) * my_live).astype(BF16).reshape(Z, D, R)
    loads[1].wait()
    snd_q[...] = turned(q_in).astype(BF16).reshape(Z, D, R)
    loads[2].wait()
    snd_kv[:, 0, :, :] = turned(k_in).astype(BF16).reshape(Z, D, R)
    loads[3].wait()
    snd_kv[:, 1, :, :] = turned(v_in).astype(BF16).reshape(Z, D, R)
    loads[4].wait()

    kgt[...] = jnp.zeros_like(kgt)
    kgt[0:T, :] = ck_in[...]
    for b in range(Z * D // R):
        kg_s1[b * R : (b + 1) * R, :] = kgt[:, b * R : (b + 1) * R].T
    my_taps = kg_s1[pl.ds(pl.multiple_of(z * D, D), D), :]
    for t in range(T):
        kb[t] = jnp.broadcast_to(my_taps[:, t : t + 1], (D, R))
    kga[...] = jnp.zeros_like(kga)
    m_run[...] = jnp.full(m_run.shape, FILL, F32)
    l_run[...] = jnp.zeros_like(l_run)
    acc[...] = jnp.zeros_like(acc)
    dq_acc[...] = jnp.zeros_like(dq_acc)
    gfc[0:D, :] = jnp.zeros((D, NQ), BF16)
    row = lax.broadcasted_iota(jnp.int32, (D, NQ), 0)
    qaug[D : 2 * D, :] = jnp.where(row == 0, 1.0, 0.0).astype(BF16)

    pl.semaphore_wait(barrier, (Z - 1) + 3 + (NDP - 1))

    def cols(j):
        return pl.ds(pl.multiple_of(j * R, R), R)

    def seq_at(ref, p):
        return ref.at[p // 2, p % 2]

    def kv_at(n, g):
        return kvt.at[n, :, :, cols(g)]

    sends = []

    def send(cp):
        cp.start()
        sends.append(cp)

    for i in zorder:
        p = (z + i) % Z
        send(rcopy(snd_g.at[p], seq_at(gseq, 1 + 2 * z + c), s_g.at[i], r_g.at[z], zpeer(p)))
    for i in zorder:
        p = (z + i) % Z
        send(rcopy(snd_q.at[p], qt.at[:, cols(z)], s_q.at[i], r_q.at[z], zpeer(p)))
    for i in zorder:
        p = (z + i) % Z
        n = slot_of[Z - i]
        send(rcopy(snd_kv.at[p], kv_at(n, gm), s_kv.at[i], r_kv.at[n], zpeer(p)))
    kvt[0, :, :, cols(gm)] = snd_kv[z]
    qt[:, cols(z)] = snd_q[z]
    gseq[(1 + 2 * z + c) // 2, (1 + 2 * z + c) % 2] = snd_g[z]

    def share(n):
        for i in range(1, 4):
            rcopy(kv_at(n, gm), kv_at(n, gm), s_grp.at[n, i], r_grp.at[n, gm], gpeer((gm + i) % 4)).start()

    share(0)

    for i in zorder:
        p = (z + i) % Z
        rcopy(snd_g.at[p], seq_at(gseq, 1 + 2 * p + c), s_g.at[i], r_g.at[p], zpeer(p)).wait_recv()

    def halo(seq, n):
        mine = seq.at[pl.ds(c, Z), 1 - c]
        rcopy(mine, mine, s_h.at[n], r_h.at[n], gpeer(gm + 1 - 2 * c)).start()

        @pl.when(x != c)
        def _():
            rcopy(
                seq.at[c * Z, 1 - c], seq.at[(1 - c) * Z, 1 - c],
                s_h.at[n + 1], r_h.at[n + 1], gpeer(3 - gm),
            ).start()

    def halo_wait(seq, n):
        mine = seq.at[pl.ds(c, Z), 1 - c]
        other = seq.at[pl.ds(1 - c, Z), c]
        cp = rcopy(mine, other, s_h.at[n], r_h.at[n], gpeer(gm + 1 - 2 * c))
        cp.wait_send()
        cp.wait_recv()

        @pl.when(x != c)
        def _():
            cp2 = rcopy(
                seq.at[c * Z, 1 - c], seq.at[c * Z, c],
                s_h.at[n + 1], r_h.at[n + 1], gpeer(3 - gm),
            )
            cp2.wait_send()
            cp2.wait_recv()

    halo(gseq, 0)

    lane = lax.broadcasted_iota(jnp.int32, (1, R), 1)

    def live_of(j):
        return ((x * 2 * Z + 2 * j + c) * R + lane < length).astype(F32)

    def window(seq, j):
        p = 1 + 2 * j + c
        parts = [seq[(p + d) // 2, (p + d) % 2].astype(F32) for d in (-1, 0, 1)]
        return jnp.concatenate(parts, axis=1), parts[1]

    def shifted(wide, s):
        if s == 0:
            return wide[:, R : 2 * R]
        return pltpu.roll(wide, (3 * R - s) % (3 * R), 1)[:, R : 2 * R]

    def grad_block(j, carry):
        wide, mid = window(gseq, j)
        total = mid
        for t in range(T):
            total = total + kb[t] * shifted(wide, HALF - t)
        dot_t[:, cols(j)] = (total * live_of(j)).astype(BF16)
        return carry

    halo_wait(gseq, 0)
    lax.fori_loop(0, Z, grad_block, 0)

    for i in zorder:
        p = (z + i) % Z
        rcopy(snd_q.at[p], qt.at[:, cols(p)], s_q.at[i], r_q.at[p], zpeer(p)).wait_recv()
    qaug[0:D, :] = (qt[...].astype(F32) * (D ** -0.5)).astype(BF16)

    lane_full = lax.broadcasted_iota(jnp.int32, (R, R), 1)
    sub_full = lax.broadcasted_iota(jnp.int32, (R, R), 0)

    def keys_at(n):
        return pl.ds(pl.multiple_of(n * CK, CK), CK)

    def forward(n, carry):
        @pl.when(n < Z)
        def _():
            rcopy(kv_at(n, gm), kv_at(n, gm), s_kv.at[0], r_kv.at[n], gpeer(gm)).wait_recv()
            share(n)

        m = n - 1
        zs = (z + off_of(m)) % Z
        for i in range(1, 4):
            g = (gm + i) % 4
            rcopy(kv_at(m, g), kv_at(m, g), s_grp.at[m, i], r_grp.at[m, g], gpeer(g)).wait_recv()
        for g in range(4):
            blk = kvt[m, :, :, g * R : (g + 1) * R].reshape(2 * D, R).astype(F32).T
            at = pl.ds(pl.multiple_of(m * CK + g * R, R), R)
            kvn[at, :] = blk.astype(BF16)
            frame = ((g // 2) * 2 * Z + 2 * zs + g % 2) * R + sub_full
            fill = jnp.where((lane_full == D) & (frame >= length), FILL, 0.0)
            kaug[at, :] = jnp.where(lane_full < D, blk, fill).astype(BF16)
        at = keys_at(m)
        s = dot(kaug[at, :], qaug[...])
        m_old = m_run[0:1, :]
        m_new = jnp.maximum(m_old, jnp.max(s, axis=0, keepdims=True))
        w = jnp.exp(s - m_new)
        alpha = jnp.exp(m_old - m_new)
        l_run[0:1, :] = l_run[0:1, :] * alpha + jnp.sum(w, axis=0, keepdims=True)
        wb = w.astype(BF16)
        w_all[at, :] = wb
        acc[...] = acc[...] * alpha + dot(kvt[m, 1], wb)
        m_run[0:1, :] = m_new
        m_all[m, 0:1, :] = m_new
        return carry

    lax.fori_loop(1, Z + 1, forward, 0)

    inv = 1.0 / l_run[0:1, :]
    l_run[0:1, :] = inv
    att = (acc[...] * inv).astype(BF16)
    for j in range(Z):
        blk = (att[:, j * R : (j + 1) * R].astype(F32) * live_of(j)).astype(BF16)
        oseq[(1 + 2 * j + c) // 2, (1 + 2 * j + c) % 2] = blk
    halo(oseq, 2)
    m_run[1:2, :] = jnp.sum(dot_t[...].astype(F32) * att.astype(F32), axis=0, keepdims=True)

    def out_block(j, carry):
        wide, mid = window(oseq, j)
        p = 1 + 2 * j + c
        grad = gseq[p // 2, p % 2].astype(F32)
        total = mid
        for t in range(T):
            seg = shifted(wide, t - HALF)
            total = total + kb[t] * seg
            kga[t] = kga[t] + grad * seg
        mix_s[j] = (total * live_of(j)).astype(BF16)
        return carry

    def mix_copy(i, p, h):
        return rcopy(mix_s.at[p], land.at[h, 0], s_m.at[i], r_m.at[h], zpeer(p))

    def taps_a(i):
        g = (gm + i) % 4
        return rcopy(kg_grp.at[gm], kg_grp.at[gm], s_kg.at[i], r_kg.at[gm], gpeer(g))

    def taps_a_in(i):
        g = (gm + i) % 4
        return rcopy(kg_grp.at[g], kg_grp.at[g], s_kg.at[i], r_kg.at[g], gpeer(g))

    def taps_b(i):
        return rcopy(kg_dp.at[dp], kg_dp.at[dp], s_kg.at[4 + i], r_kg.at[4 + dp], ((dp + i) % NDP, me))

    def taps_b_in(i):
        p = (dp + i) % NDP
        return rcopy(kg_dp.at[p], kg_dp.at[p], s_kg.at[4 + i], r_kg.at[4 + p], (p, me))

    def taps_c(i, p, h):
        return rcopy(kg_s, kg_land.at[h], s_kg.at[4 + NDP + i], r_kg.at[4 + NDP + h], zpeer(p))

    def part_copy(n, i):
        g = (gm + i) % 4
        return rcopy(part.at[n, :, :, cols(g)], gred.at[n, gm], s_p.at[n, i], r_p.at[n, gm], gpeer(g))

    def part_in(n, i):
        g = (gm + i) % 4
        return rcopy(part.at[n, :, :, cols(g)], gred.at[n, g], s_p.at[n, i], r_p.at[n, g], gpeer(g))

    def add_up(n):
        for i in range(1, 4):
            part_in(n, i).wait_recv()
        gred[n, gm] = part[n, :, :, cols(gm)]
        total = (gred[n, 0].astype(F32) + gred[n, 1].astype(F32)) + (
            gred[n, 2].astype(F32) + gred[n, 3].astype(F32)
        )
        kv_s[n] = total.astype(BF16)

    def kv_copy(n, h):
        return rcopy(kv_s.at[n], land.at[h, pl.ds(2, 2)], s_o.at[n], r_o.at[h], zpeer((z + off_of(n)) % Z))

    def backward(k, carry):
        n = Z - 1 - k
        at = keys_at(n)
        f = jnp.exp(m_all[n, 0:1, :] - m_run[0:1, :]) * l_run[0:1, :]
        gf = (dot_t[...].astype(F32) * f).astype(BF16)
        gfc[D : 2 * D, :] = gf
        dp_t = dot(kvn[at, :], gfc[...])
        wb = w_all[at, :]
        ds = (wb.astype(F32) * (dp_t - m_run[1:2, :] * f)).astype(BF16)
        part[n, 0] = (dot(qt[...], ds, NT) * (D ** -0.5)).astype(BF16)
        part[n, 1] = dot(gf, wb, NT).astype(BF16)
        for i in range(1, 4):
            part_copy(n, i).start()
        dq_acc[...] = dq_acc[...] + dot(kvt[n, 0], ds)

        @pl.when(k > 0)
        def _():
            add_up(n + 1)
            kv_copy(n + 1, z).start()

        @pl.when(k == 0)
        def _():
            halo_wait(oseq, 2)
            lax.fori_loop(0, Z, out_block, 0)
            for i in zorder:
                mix_copy(i, (z + i) % Z, z).start()
            lane_d = lax.broadcasted_iota(jnp.int32, (D, R), 1)
            red = jnp.zeros((D, R), F32)
            for t in range(T):
                red = jnp.where(lane_d == t, jnp.sum(kga[t], axis=1, keepdims=True), red)
            kg_grp[gm] = jnp.concatenate([red, jnp.zeros((R - D, R), F32)], axis=0).T[0:32, :]
            for i in range(1, 4):
                taps_a(i).start()

        @pl.when(k == (Z + 1) // 3)
        def _():
            for i in range(1, 4):
                taps_a_in(i).wait_recv()
            kg_dp[dp] = (kg_grp[0] + kg_grp[1]) + (kg_grp[2] + kg_grp[3])
            for i in range(1, NDP):
                taps_b(i).start()

        @pl.when(k == Z - 2)
        def _():
            for i in range(1, NDP):
                taps_b_in(i).wait_recv()
            total = kg_dp[0]
            for i in range(1, NDP):
                total = total + kg_dp[i]
            kg_s[...] = total
            for i in zorder:
                taps_c(i, (z + i) % Z, z).start()

        return carry

    lax.fori_loop(0, Z, backward, 0)

    for j in range(Z):
        dq_s[j] = (dq_acc[:, j * R : (j + 1) * R] * (D ** -0.5)).astype(BF16)

    def dq_copy(i, p, h):
        return rcopy(dq_s.at[p], land.at[h, 1], s_dq.at[i], r_dq.at[h], zpeer(p))

    for i in zorder:
        dq_copy(i, (z + i) % Z, z).start()
    add_up(0)
    local = [
        pltpu.make_async_copy(mix_s.at[z], land.at[z, 0], s_loc.at[0]),
        pltpu.make_async_copy(dq_s.at[z], land.at[z, 1], s_loc.at[1]),
        pltpu.make_async_copy(kv_s.at[0], land.at[z, pl.ds(2, 2)], s_loc.at[2]),
        pltpu.make_async_copy(kg_s, kg_land.at[z], s_loc.at[3]),
    ]
    for cp in local:
        cp.start()

    for cp in sends:
        cp.wait_send()

    def drain(n, carry):
        for i in range(1, 4):
            rcopy(kv_at(n, gm), kv_at(n, gm), s_grp.at[n, i], r_grp.at[n, gm], gpeer((gm + i) % 4)).wait_send()
            part_copy(n, i).wait_send()
        return carry

    lax.fori_loop(0, Z, drain, 0)
    for i in range(1, 4):
        taps_a(i).wait_send()
    for i in range(1, NDP):
        taps_b(i).wait_send()
    for i in zorder:
        p = (z + i) % Z
        for cp in (mix_copy(i, p, p), taps_c(i, p, p), dq_copy(i, p, p)):
            cp.wait_send()
            cp.wait_recv()
        kv_copy(slot_of[i], p).wait_send()
        kv_copy(slot_of[i], p).wait_recv()
    for cp in local:
        cp.wait()


def finish(Z, T, land, kg, mix_out, dq_out, dk_out, dv_out, kg_out):
    for n, out in enumerate((mix_out, dq_out, dk_out, dv_out)):
        out[...] = land[:, n].astype(F32).reshape(Z * D, R).T.astype(BF16)
    for h in range(0, Z, 2):
        both = jnp.concatenate([kg[h][0:T, 0:D], kg[h + 1][0:T, 0:D]], axis=1)
        kg_out[:, h * D : (h + 2) * D] = both


def per_device(Z, NDP, lengths, q, k, v, g, taps):
    W = Z * D
    NQ = R * Z
    NK = 4 * NQ
    T = taps.shape[0]
    CK = 4 * R
    vm = pltpu.VMEM
    dma = pltpu.SemaphoreType.DMA
    scratch = [
        vm((R, W), BF16), vm((R, W), BF16), vm((R, W), BF16), vm((R, W), BF16), vm((T, W), F32),
        vm((Z, 2, D, R), BF16), vm((Z, D, R), BF16), vm((Z, D, R), BF16),
        vm((Z, 2, D, CK), BF16), vm((NK, 2 * D), BF16), vm((NK, 2 * D), BF16),
        vm((D, NQ), BF16), vm((2 * D, NQ), BF16),
        vm((Z + 1, 2, D, R), BF16), vm((Z + 1, 2, D, R), BF16),
        vm((D, NQ), BF16), vm((2 * D, NQ), BF16),
        vm((T, D, R), F32), vm((T, D, R), F32), vm((R, W), F32),
        vm((4, 32, R), F32), vm((NDP, 32, R), F32), vm((32, R), F32), vm((W, R), F32),
        vm((NK, NQ), BF16), vm((Z, 8, NQ), F32), vm((8, NQ), F32), vm((8, NQ), F32),
        vm((D, NQ), F32), vm((D, NQ), F32),
        vm((Z, D, R), BF16), vm((Z, D, R), BF16),
        vm((Z, 2, D, CK), BF16), vm((Z, 4, 2, D, R), BF16), vm((Z, 2, D, R), BF16),
        dma((5,)),
        dma((Z,)), dma((Z,)), dma((Z,)), dma((Z,)), dma((Z,)), dma((Z,)),
        dma((Z, 4)), dma((Z, 4)), dma((4,)), dma((4,)),
        dma((4 + NDP + Z,)), dma((4 + NDP + Z,)), dma((Z,)), dma((Z,)), dma((Z,)), dma((Z,)),
        dma((Z, 4)), dma((Z, 4)), dma((Z,)), dma((Z,)), dma((4,)),
    ]
    vspec = pl.BlockSpec(memory_space=pltpu.VMEM)
    anyspec = pl.BlockSpec(memory_space=pl.ANY)
    land, kg = pl.pallas_call(
        functools.partial(kernel, Z, NDP),
        out_shape=(
            jax.ShapeDtypeStruct((Z, 4, D, R), BF16),
            jax.ShapeDtypeStruct((Z, 32, R), F32),
        ),
        in_specs=[pl.BlockSpec(memory_space=pltpu.SMEM)] + [anyspec] * 5,
        out_specs=(anyspec, anyspec),
        scratch_shapes=scratch,
        compiler_params=pltpu.CompilerParams(
            collective_id=0, has_side_effects=True, vmem_limit_bytes=56 * 1024 * 1024
        ),
        cost_estimate=pl.CostEstimate(
            flops=12 * NQ * NK * D, bytes_accessed=9 * R * W * 2, transcendentals=NQ * NK
        ),
    )(lengths, q[0], k[0], v[0], g[0], taps)
    outs = pl.pallas_call(
        functools.partial(finish, Z, T),
        out_shape=(
            jax.ShapeDtypeStruct((R, W), BF16), jax.ShapeDtypeStruct((R, W), BF16),
            jax.ShapeDtypeStruct((R, W), BF16), jax.ShapeDtypeStruct((R, W), BF16),
            jax.ShapeDtypeStruct((T, W), F32),
        ),
        in_specs=[vspec] * 2,
        out_specs=(vspec,) * 5,
    )(land, kg)
    return outs[0][None], outs[1][None], outs[2][None], outs[3][None], outs[4]


def solution(mesh):
    Z = mesh.shape["ctx"] // 4
    NDP = mesh.shape["dp"]
    split = P("dp", "ctx", None)
    return jax.shard_map(
        functools.partial(per_device, Z, NDP),
        mesh=mesh,
        in_specs=(P(), split, split, split, split, P()),
        out_specs=(split, split, split, split, P()),
        check_vma=False,
    )
```

```python
import functools

import jax
import jax.numpy as jnp
from jax import lax
from jax.experimental import pallas as pl
from jax.experimental.pallas import tpu as pltpu
from jax.sharding import PartitionSpec as P

MESH = pl.DeviceIdType.MESH
D = 64
R = 128
FILL = -1e30
F32 = jnp.float32
BF16 = jnp.bfloat16

NN = (((1,), (0,)), ((), ()))
NT = (((1,), (1,)), ((), ()))


def dot(a, b, dims=NN):
    return lax.dot_general(a, b, dims, preferred_element_type=F32)


def kernel(
    Z, NDP,
    len_ref, q_hbm, k_hbm, v_hbm, g_hbm, ck_hbm,
    land, kg_land,
    q_in, k_in, v_in, g_in, ck_in,
    snd_kv, snd_q, snd_g, snd_d, gx, gh, gbuf, kvt, kvn, kaug, qt, qaug, oseq, dot_t, gfc,
    kb, kga, kgt, kg_grp, kg_dp, kg_s, kg_s1,
    w_all, m_all, m_run, l_run, acc, dq_acc, mix_s, dq_s, part, gred, kv_s,
    s_in, s_kv, r_kv, s_q, r_q, s_g, r_g, s_d, r_d, s_grp, r_grp, s_h, r_h,
    s_kg, r_kg, s_m, r_m, s_dq, r_dq, s_p, r_p, s_o, r_o, s_loc,
):
    NQ = R * Z
    CK = 4 * R
    T = ck_in.shape[0]
    HALF = (T - 1) // 2
    me = lax.axis_index("ctx")
    dp = lax.axis_index("dp")
    x = me // (2 * Z)
    z = (me // 2) % Z
    c = me % 2
    gm = 2 * x + c
    N = 4 * Z
    sib = gm + 1 - 2 * c
    across = (gm + 2) % 4
    across_sib = 3 - gm
    length = len_ref[dp]

    def zpeer(p):
        return (dp, x * 2 * Z + 2 * p + c)

    def gpeer(g):
        return (dp, (g // 2) * 2 * Z + 2 * z + g % 2)

    def rcopy(src, dst, ssem, rsem, dev):
        return pltpu.make_async_remote_copy(
            src_ref=src, dst_ref=dst, send_sem=ssem, recv_sem=rsem, device_id=dev, device_id_type=MESH
        )

    offs = [0]
    for i in range(1, Z // 2 + 1):
        offs.append(i)
        if Z - i != i:
            offs.append(Z - i)
    zorder = offs[1:]
    slot_of = {o: n for n, o in enumerate(offs)}

    def off_of(n):
        odd = n % 2
        return odd * ((n + 1) // 2) + (1 - odd) * ((Z - n // 2) % Z)

    zero_blk = jnp.zeros((D, R), BF16)
    oseq[0, 0] = zero_blk
    oseq[Z, 1] = zero_blk

    barrier = pltpu.get_barrier_semaphore()
    for i in range(1, Z):
        pl.semaphore_signal(barrier, inc=1, device_id=zpeer((z + i) % Z), device_id_type=MESH)
    for i in range(1, 4):
        pl.semaphore_signal(barrier, inc=1, device_id=gpeer((gm + i) % 4), device_id_type=MESH)
    for i in range(1, NDP):
        pl.semaphore_signal(barrier, inc=1, device_id=((dp + i) % NDP, me), device_id_type=MESH)
    pl.semaphore_signal(barrier, inc=1, device_id=(dp, (me + 2 * c - 1 + N) % N), device_id_type=MESH)

    loads = []
    for n, (a, b) in enumerate(((q_hbm, q_in), (k_hbm, k_in), (v_hbm, v_in), (g_hbm, g_in), (ck_hbm, ck_in))):
        cp = pltpu.make_async_copy(a, b, s_in.at[n])
        cp.start()
        loads.append(cp)

    turned = lambda a: a.astype(F32).T.astype(BF16).reshape(Z, D, R)
    loads[0].wait()
    snd_q[...] = turned(q_in[...])
    loads[1].wait()
    snd_kv[:, 0, :, :] = turned(k_in[...])
    loads[2].wait()
    snd_kv[:, 1, :, :] = turned(v_in[...])
    loads[3].wait()
    loads[4].wait()

    pl.semaphore_wait(barrier, (Z - 1) + 3 + (NDP - 1) + 1)

    def cols(j):
        return pl.ds(pl.multiple_of(j * R, R), R)

    def seq_at(ref, p):
        return ref.at[p // 2, p % 2]

    def kv_at(n, g):
        return kvt.at[n, :, :, cols(g)]

    sends = []

    def send(cp):
        cp.start()
        sends.append(cp)

    up, down = (dp, (me + 1) % N), (dp, (me + N - 1) % N)
    send(rcopy(g_in.at[pl.ds(R - 16, 16)], gh.at[0], s_h.at[0], r_h.at[0], up))
    send(rcopy(g_in.at[pl.ds(0, 16)], gh.at[1], s_h.at[1], r_h.at[1], down))
    for i in zorder:
        p = (z + i) % Z
        send(rcopy(snd_q.at[p], qt.at[:, cols(z)], s_q.at[i], r_q.at[z], zpeer(p)))
    for i in zorder:
        p = (z + i) % Z
        n = slot_of[Z - i]
        send(rcopy(snd_kv.at[p], kv_at(n, gm), s_kv.at[i], r_kv.at[n], zpeer(p)))
    kvt[0, :, :, cols(gm)] = snd_kv[z]

    def grp_copy(n, g, k, to):
        return rcopy(kv_at(n, g), kv_at(n, g), s_grp.at[n, k], r_grp.at[n, g], gpeer(to))

    def share(n):
        grp_copy(n, gm, 1, across).start()
        grp_copy(n, gm, 0, sib).start()

    def relay(n):
        grp_copy(n, across, 1, across).wait_recv()
        grp_copy(n, across, 2, sib).start()

    share(0)
    qt[:, cols(z)] = snd_q[z]

    kgt[...] = jnp.zeros_like(kgt)
    kgt[0:T, :] = ck_in[...]
    for b in range(Z * D // R):
        kg_s1[b * R : (b + 1) * R, :] = kgt[:, b * R : (b + 1) * R].T
    my_taps = kg_s1[pl.ds(pl.multiple_of(z * D, D), D), :]
    for t in range(T):
        kb[t] = jnp.broadcast_to(my_taps[:, t : t + 1], (D, R))
    kga[...] = jnp.zeros_like(kga)
    m_run[...] = jnp.full(m_run.shape, FILL, F32)
    l_run[...] = jnp.zeros_like(l_run)
    acc[...] = jnp.zeros_like(acc)
    dq_acc[...] = jnp.zeros_like(dq_acc)
    gfc[0:D, :] = jnp.zeros((D, NQ), BF16)
    row = lax.broadcasted_iota(jnp.int32, (D, NQ), 0)
    qaug[D : 2 * D, :] = jnp.where(row == 0, 1.0, 0.0).astype(BF16)

    def live_rows(first, count):
        frame = first + lax.broadcasted_iota(jnp.int32, (count, 1), 0)
        return ((frame >= 0) & (frame < length)).astype(F32)

    own_live = live_rows(me * R, R)
    own = g_in[...].astype(F32) * own_live
    gx[16 : 16 + R, :] = own
    snd_g[...] = turned(own)
    rcopy(g_in.at[pl.ds(R - 16, 16)], gh.at[0], s_h.at[0], r_h.at[0], up).wait_recv()
    rcopy(g_in.at[pl.ds(0, 16)], gh.at[1], s_h.at[1], r_h.at[1], down).wait_recv()
    gx[0:16, :] = jnp.where(live_rows(me * R - 16, 16) > 0, gh[0].astype(F32), 0.0)
    gx[16 + R : 32 + R, :] = jnp.where(live_rows(me * R + R, 16) > 0, gh[1].astype(F32), 0.0)

    def grad_block(b, carry):
        at = cols(b)
        total = gx[16 : 16 + R, at]
        for t in range(T):
            total = total + ck_in[t : t + 1, at] * gx[pl.ds(16 + HALF - t, R), at]
        gx2 = (total * own_live).T.astype(BF16)
        for h in range(R // D):
            snd_d[(R // D) * b + h] = gx2[h * D : (h + 1) * D]
        return carry

    lax.fori_loop(0, Z * D // R, grad_block, 0)
    for i in zorder:
        p = (z + i) % Z
        send(rcopy(snd_d.at[p], dot_t.at[:, cols(z)], s_d.at[i], r_d.at[z], zpeer(p)))
    for i in zorder:
        p = (z + i) % Z
        send(rcopy(snd_g.at[p], gbuf.at[z], s_g.at[i], r_g.at[z], zpeer(p)))
    dot_t[:, cols(z)] = snd_d[z]
    gbuf[z] = snd_g[z]

    def halo(seq, n):
        mine = seq.at[pl.ds(c, Z), 1 - c]
        rcopy(mine, mine, s_h.at[n], r_h.at[n], gpeer(gm + 1 - 2 * c)).start()

        @pl.when(x != c)
        def _():
            rcopy(
                seq.at[c * Z, 1 - c], seq.at[(1 - c) * Z, 1 - c],
                s_h.at[n + 1], r_h.at[n + 1], gpeer(3 - gm),
            ).start()

    def halo_wait(seq, n):
        mine = seq.at[pl.ds(c, Z), 1 - c]
        other = seq.at[pl.ds(1 - c, Z), c]
        cp = rcopy(mine, other, s_h.at[n], r_h.at[n], gpeer(gm + 1 - 2 * c))
        cp.wait_send()
        cp.wait_recv()

        @pl.when(x != c)
        def _():
            cp2 = rcopy(
                seq.at[c * Z, 1 - c], seq.at[c * Z, c],
                s_h.at[n + 1], r_h.at[n + 1], gpeer(3 - gm),
            )
            cp2.wait_send()
            cp2.wait_recv()

    lane = lax.broadcasted_iota(jnp.int32, (1, R), 1)

    def live_of(j):
        return ((x * 2 * Z + 2 * j + c) * R + lane < length).astype(F32)

    def window(seq, j):
        p = 1 + 2 * j + c
        parts = [seq[(p + d) // 2, (p + d) % 2].astype(F32) for d in (-1, 0, 1)]
        return jnp.concatenate(parts, axis=1), parts[1]

    def shifted(wide, s):
        if s == 0:
            return wide[:, R : 2 * R]
        return pltpu.roll(wide, (3 * R - s) % (3 * R), 1)[:, R : 2 * R]

    for i in zorder:
        p = (z + i) % Z
        rcopy(snd_q.at[p], qt.at[:, cols(p)], s_q.at[i], r_q.at[p], zpeer(p)).wait_recv()
    qaug[0:D, :] = (qt[...].astype(F32) * (D ** -0.5)).astype(BF16)

    lane_full = lax.broadcasted_iota(jnp.int32, (R, R), 1)
    sub_full = lax.broadcasted_iota(jnp.int32, (R, R), 0)

    def keys_at(n):
        return pl.ds(pl.multiple_of(n * CK, CK), CK)

    def arrive(n):
        rcopy(kv_at(n, gm), kv_at(n, gm), s_kv.at[0], r_kv.at[n], gpeer(across)).wait_recv()
        share(n)

    arrive(1)
    relay(0)

    def forward(n, carry):
        @pl.when(n < Z)
        def _():
            arrive(n)

        @pl.when(n <= Z)
        def _():
            relay(n - 1)

        m = n - 2
        zs = (z + off_of(m)) % Z
        grp_copy(m, sib, 0, sib).wait_recv()
        grp_copy(m, across_sib, 2, sib).wait_recv()
        for g in range(4):
            blk = kvt[m, :, :, g * R : (g + 1) * R].reshape(2 * D, R).astype(F32).T
            at = pl.ds(pl.multiple_of(m * CK + g * R, R), R)
            kvn[at, :] = blk.astype(BF16)
            frame = ((g // 2) * 2 * Z + 2 * zs + g % 2) * R + sub_full
            fill = jnp.where((lane_full == D) & (frame >= length), FILL, 0.0)
            kaug[at, :] = jnp.where(lane_full < D, blk, fill).astype(BF16)
        at = keys_at(m)
        s = dot(kaug[at, :], qaug[...])
        m_old = m_run[0:1, :]
        m_new = jnp.maximum(m_old, jnp.max(s, axis=0, keepdims=True))
        w = jnp.exp(s - m_new)
        alpha = jnp.exp(m_old - m_new)
        l_run[0:1, :] = l_run[0:1, :] * alpha + jnp.sum(w, axis=0, keepdims=True)
        wb = w.astype(BF16)
        w_all[at, :] = wb
        acc[...] = acc[...] * alpha + dot(kvt[m, 1], wb)
        m_run[0:1, :] = m_new
        m_all[m, 0:1, :] = m_new
        return carry

    lax.fori_loop(2, Z + 2, forward, 0)

    for i in zorder:
        p = (z + i) % Z
        rcopy(snd_d.at[p], dot_t.at[:, cols(p)], s_d.at[i], r_d.at[p], zpeer(p)).wait_recv()


    inv = 1.0 / l_run[0:1, :]
    l_run[0:1, :] = inv
    att = (acc[...] * inv).astype(BF16)
    for j in range(Z):
        blk = (att[:, j * R : (j + 1) * R].astype(F32) * live_of(j)).astype(BF16)
        oseq[(1 + 2 * j + c) // 2, (1 + 2 * j + c) % 2] = blk
    halo(oseq, 2)
    m_run[1:2, :] = jnp.sum(dot_t[...].astype(F32) * att.astype(F32), axis=0, keepdims=True)

    def out_block(j, carry):
        wide, mid = window(oseq, j)
        grad = gbuf[j].astype(F32)
        total = mid
        for t in range(T):
            seg = shifted(wide, t - HALF)
            total = total + kb[t] * seg
            kga[t] = kga[t] + grad * seg
        mix_s[j] = (total * live_of(j)).astype(BF16)
        return carry

    def mix_copy(i, p, h):
        return rcopy(mix_s.at[p], land.at[h, 0], s_m.at[i], r_m.at[h], zpeer(p))

    def taps_a(i):
        g = (gm + i) % 4
        return rcopy(kg_grp.at[gm], kg_grp.at[gm], s_kg.at[i], r_kg.at[gm], gpeer(g))

    def taps_a_in(i):
        g = (gm + i) % 4
        return rcopy(kg_grp.at[g], kg_grp.at[g], s_kg.at[i], r_kg.at[g], gpeer(g))

    def taps_b(i):
        return rcopy(kg_dp.at[dp], kg_dp.at[dp], s_kg.at[4 + i], r_kg.at[4 + dp], ((dp + i) % NDP, me))

    def taps_b_in(i):
        p = (dp + i) % NDP
        return rcopy(kg_dp.at[p], kg_dp.at[p], s_kg.at[4 + i], r_kg.at[4 + p], (p, me))

    def taps_c(i, p, h):
        return rcopy(kg_s, kg_land.at[h], s_kg.at[4 + NDP + i], r_kg.at[4 + NDP + h], zpeer(p))

    def part_copy(n, i):
        g = (gm + i) % 4
        return rcopy(part.at[n, :, :, cols(g)], gred.at[n, gm], s_p.at[n, i], r_p.at[n, gm], gpeer(g))

    def part_in(n, i):
        g = (gm + i) % 4
        return rcopy(part.at[n, :, :, cols(g)], gred.at[n, g], s_p.at[n, i], r_p.at[n, g], gpeer(g))

    def add_up(n):
        for i in range(1, 4):
            part_in(n, i).wait_recv()
        gred[n, gm] = part[n, :, :, cols(gm)]
        total = (gred[n, 0].astype(F32) + gred[n, 1].astype(F32)) + (
            gred[n, 2].astype(F32) + gred[n, 3].astype(F32)
        )
        kv_s[n] = total.astype(BF16)

    def kv_copy(n, h):
        return rcopy(kv_s.at[n], land.at[h, pl.ds(2, 2)], s_o.at[n], r_o.at[h], zpeer((z + off_of(n)) % Z))

    def backward(k, carry):
        n = Z - 1 - k
        at = keys_at(n)
        f = jnp.exp(m_all[n, 0:1, :] - m_run[0:1, :]) * l_run[0:1, :]
        gf = (dot_t[...].astype(F32) * f).astype(BF16)
        gfc[D : 2 * D, :] = gf
        dp_t = dot(kvn[at, :], gfc[...])
        wb = w_all[at, :]
        ds = (wb.astype(F32) * (dp_t - m_run[1:2, :] * f)).astype(BF16)
        part[n, 0] = (dot(qt[...], ds, NT) * (D ** -0.5)).astype(BF16)
        part[n, 1] = dot(gf, wb, NT).astype(BF16)
        for i in range(1, 4):
            part_copy(n, i).start()
        dq_acc[...] = dq_acc[...] + dot(kvt[n, 0], ds)

        @pl.when(k > 1)
        def _():
            add_up(n + 2)
            kv_copy(n + 2, z).start()

        @pl.when(k == 0)
        def _():
            for i in zorder:
                p = (z + i) % Z
                rcopy(snd_g.at[p], gbuf.at[p], s_g.at[i], r_g.at[p], zpeer(p)).wait_recv()
            halo_wait(oseq, 2)
            lax.fori_loop(0, Z, out_block, 0)
            for i in zorder:
                mix_copy(i, (z + i) % Z, z).start()
            lane_d = lax.broadcasted_iota(jnp.int32, (D, R), 1)
            red = jnp.zeros((D, R), F32)
            for t in range(T):
                red = jnp.where(lane_d == t, jnp.sum(kga[t], axis=1, keepdims=True), red)
            kg_grp[gm] = jnp.concatenate([red, jnp.zeros((R - D, R), F32)], axis=0).T[0:32, :]
            for i in range(1, 4):
                taps_a(i).start()

        @pl.when(k == min(4, Z - 1))
        def _():
            for i in range(1, 4):
                taps_a_in(i).wait_recv()
            kg_dp[dp] = (kg_grp[0] + kg_grp[1]) + (kg_grp[2] + kg_grp[3])
            for i in range(1, NDP):
                taps_b(i).start()

        return carry

    lax.fori_loop(0, Z, backward, 0)

    for j in range(Z):
        dq_s[j] = (dq_acc[:, j * R : (j + 1) * R] * (D ** -0.5)).astype(BF16)

    def dq_copy(i, p, h):
        return rcopy(dq_s.at[p], land.at[h, 1], s_dq.at[i], r_dq.at[h], zpeer(p))

    for i in zorder:
        dq_copy(i, (z + i) % Z, z).start()
    add_up(1)
    kv_copy(1, z).start()
    for i in range(1, NDP):
        taps_b_in(i).wait_recv()
    total = kg_dp[0]
    for i in range(1, NDP):
        total = total + kg_dp[i]
    kg_s[...] = total
    for i in zorder:
        taps_c(i, (z + i) % Z, z).start()
    add_up(0)
    local = [
        pltpu.make_async_copy(mix_s.at[z], land.at[z, 0], s_loc.at[0]),
        pltpu.make_async_copy(dq_s.at[z], land.at[z, 1], s_loc.at[1]),
        pltpu.make_async_copy(kv_s.at[0], land.at[z, pl.ds(2, 2)], s_loc.at[2]),
        pltpu.make_async_copy(kg_s, kg_land.at[z], s_loc.at[3]),
    ]
    for cp in local:
        cp.start()

    for cp in sends:
        cp.wait_send()

    def drain(n, carry):
        grp_copy(n, gm, 0, sib).wait_send()
        grp_copy(n, gm, 1, across).wait_send()
        grp_copy(n, across, 2, sib).wait_send()
        for i in range(1, 4):
            part_copy(n, i).wait_send()
        return carry

    lax.fori_loop(0, Z, drain, 0)
    for i in range(1, 4):
        taps_a(i).wait_send()
    for i in range(1, NDP):
        taps_b(i).wait_send()
    for i in zorder:
        p = (z + i) % Z
        for cp in (mix_copy(i, p, p), taps_c(i, p, p), dq_copy(i, p, p)):
            cp.wait_send()
            cp.wait_recv()
        kv_copy(slot_of[i], p).wait_send()
        kv_copy(slot_of[i], p).wait_recv()
    for cp in local:
        cp.wait()


def finish(Z, T, land, kg, mix_out, dq_out, dk_out, dv_out, kg_out):
    for n, out in enumerate((mix_out, dq_out, dk_out, dv_out)):
        out[...] = land[:, n].astype(F32).reshape(Z * D, R).T.astype(BF16)
    for h in range(0, Z, 2):
        both = jnp.concatenate([kg[h][0:T, 0:D], kg[h + 1][0:T, 0:D]], axis=1)
        kg_out[:, h * D : (h + 2) * D] = both


def per_device(Z, NDP, lengths, q, k, v, g, taps):
    W = Z * D
    NQ = R * Z
    NK = 4 * NQ
    T = taps.shape[0]
    CK = 4 * R
    vm = pltpu.VMEM
    dma = pltpu.SemaphoreType.DMA
    scratch = [
        vm((R, W), BF16), vm((R, W), BF16), vm((R, W), BF16), vm((R, W), BF16), vm((T, W), F32),
        vm((Z, 2, D, R), BF16), vm((Z, D, R), BF16), vm((Z, D, R), BF16), vm((Z, D, R), BF16),
        vm((R + 32, W), F32), vm((2, 16, W), BF16), vm((Z, D, R), BF16),
        vm((Z, 2, D, CK), BF16), vm((NK, 2 * D), BF16), vm((NK, 2 * D), BF16),
        vm((D, NQ), BF16), vm((2 * D, NQ), BF16),
        vm((Z + 1, 2, D, R), BF16),
        vm((D, NQ), BF16), vm((2 * D, NQ), BF16),
        vm((T, D, R), F32), vm((T, D, R), F32), vm((R, W), F32),
        vm((4, 32, R), F32), vm((NDP, 32, R), F32), vm((32, R), F32), vm((W, R), F32),
        vm((NK, NQ), BF16), vm((Z, 8, NQ), F32), vm((8, NQ), F32), vm((8, NQ), F32),
        vm((D, NQ), F32), vm((D, NQ), F32),
        vm((Z, D, R), BF16), vm((Z, D, R), BF16),
        vm((Z, 2, D, CK), BF16), vm((Z, 4, 2, D, R), BF16), vm((Z, 2, D, R), BF16),
        dma((5,)),
        dma((Z,)), dma((Z,)), dma((Z,)), dma((Z,)), dma((Z,)), dma((Z,)), dma((Z,)), dma((Z,)),
        dma((Z, 4)), dma((Z, 4)), dma((4,)), dma((4,)),
        dma((4 + NDP + Z,)), dma((4 + NDP + Z,)), dma((Z,)), dma((Z,)), dma((Z,)), dma((Z,)),
        dma((Z, 4)), dma((Z, 4)), dma((Z,)), dma((Z,)), dma((4,)),
    ]
    vspec = pl.BlockSpec(memory_space=pltpu.VMEM)
    anyspec = pl.BlockSpec(memory_space=pl.ANY)
    land, kg = pl.pallas_call(
        functools.partial(kernel, Z, NDP),
        out_shape=(
            jax.ShapeDtypeStruct((Z, 4, D, R), BF16),
            jax.ShapeDtypeStruct((Z, 32, R), F32),
        ),
        in_specs=[pl.BlockSpec(memory_space=pltpu.SMEM)] + [anyspec] * 5,
        out_specs=(anyspec, anyspec),
        scratch_shapes=scratch,
        compiler_params=pltpu.CompilerParams(
            collective_id=0, has_side_effects=True, vmem_limit_bytes=56 * 1024 * 1024
        ),
        cost_estimate=pl.CostEstimate(
            flops=12 * NQ * NK * D, bytes_accessed=9 * R * W * 2, transcendentals=NQ * NK
        ),
    )(lengths, q[0], k[0], v[0], g[0], taps)
    outs = pl.pallas_call(
        functools.partial(finish, Z, T),
        out_shape=(
            jax.ShapeDtypeStruct((R, W), BF16), jax.ShapeDtypeStruct((R, W), BF16),
            jax.ShapeDtypeStruct((R, W), BF16), jax.ShapeDtypeStruct((R, W), BF16),
            jax.ShapeDtypeStruct((T, W), F32),
        ),
        in_specs=[vspec] * 2,
        out_specs=(vspec,) * 5,
    )(land, kg)
    return outs[0][None], outs[1][None], outs[2][None], outs[3][None], outs[4]


def solution(mesh):
    Z = mesh.shape["ctx"] // 4
    NDP = mesh.shape["dp"]
    split = P("dp", "ctx", None)
    return jax.shard_map(
        functools.partial(per_device, Z, NDP),
        mesh=mesh,
        in_specs=(P(), split, split, split, split, P()),
        out_specs=(split, split, split, split, P()),
        check_vma=False,
    )
```

```python
import functools

import jax
import jax.numpy as jnp
from jax import lax
from jax.experimental import pallas as pl
from jax.experimental.pallas import tpu as pltpu
from jax.sharding import PartitionSpec as P

MESH = pl.DeviceIdType.MESH
D = 64
R = 128
FILL = -1e30
F32 = jnp.float32
BF16 = jnp.bfloat16

NN = (((1,), (0,)), ((), ()))
NT = (((1,), (1,)), ((), ()))


def dot(a, b, dims=NN):
    return lax.dot_general(a, b, dims, preferred_element_type=F32)


def kernel(
    Z, NDP,
    len_ref, q_hbm, k_hbm, v_hbm, g_hbm, ck_hbm,
    land, kg_land,
    q_in, k_in, v_in, g_in, ck_in,
    snd_kv, snd_q, snd_g, snd_d, gx, gh, gbuf, kvt, kvn, kaug, qt, qaug, oseq, dot_t, gfc,
    kb, kga, kgt, kg_grp, kg_dp, kg_s, kg_s1,
    w_all, m_all, m_run, l_run, acc, dq_acc, mix_s, dq_s, part, gred, kv_s,
    s_in, s_kv, r_kv, s_q, r_q, s_g, r_g, s_d, r_d, s_grp, r_grp, s_h, r_h,
    s_kg, r_kg, s_m, r_m, s_dq, r_dq, s_p, r_p, s_o, r_o, s_loc,
):
    NQ = R * Z
    CK = 4 * R
    T = ck_in.shape[0]
    HALF = (T - 1) // 2
    me = lax.axis_index("ctx")
    dp = lax.axis_index("dp")
    x = me // (2 * Z)
    z = (me // 2) % Z
    c = me % 2
    gm = 2 * x + c
    N = 4 * Z
    sib = gm + 1 - 2 * c
    across = (gm + 2) % 4
    across_sib = 3 - gm
    length = len_ref[dp]

    def zpeer(p):
        return (dp, x * 2 * Z + 2 * p + c)

    def gpeer(g):
        return (dp, (g // 2) * 2 * Z + 2 * z + g % 2)

    def rcopy(src, dst, ssem, rsem, dev):
        return pltpu.make_async_remote_copy(
            src_ref=src, dst_ref=dst, send_sem=ssem, recv_sem=rsem, device_id=dev, device_id_type=MESH
        )

    offs = [0]
    for i in range(1, Z // 2 + 1):
        offs.append(i)
        if Z - i != i:
            offs.append(Z - i)
    zorder = offs[1:]
    slot_of = {o: n for n, o in enumerate(offs)}

    def off_of(n):
        odd = n % 2
        return odd * ((n + 1) // 2) + (1 - odd) * ((Z - n // 2) % Z)

    zero_blk = jnp.zeros((D, R), BF16)
    oseq[0, 0] = zero_blk
    oseq[Z, 1] = zero_blk

    barrier = pltpu.get_barrier_semaphore()
    for i in range(1, Z):
        pl.semaphore_signal(barrier, inc=1, device_id=zpeer((z + i) % Z), device_id_type=MESH)
    for i in range(1, 4):
        pl.semaphore_signal(barrier, inc=1, device_id=gpeer((gm + i) % 4), device_id_type=MESH)
    for i in range(1, NDP):
        pl.semaphore_signal(barrier, inc=1, device_id=((dp + i) % NDP, me), device_id_type=MESH)
    pl.semaphore_signal(barrier, inc=1, device_id=(dp, (me + 2 * c - 1 + N) % N), device_id_type=MESH)

    loads = []
    for n, (a, b) in enumerate(((q_hbm, q_in), (k_hbm, k_in), (v_hbm, v_in), (g_hbm, g_in), (ck_hbm, ck_in))):
        cp = pltpu.make_async_copy(a, b, s_in.at[n])
        cp.start()
        loads.append(cp)

    turned = lambda a: a.astype(F32).T.astype(BF16).reshape(Z, D, R)
    loads[0].wait()
    snd_q[...] = turned(q_in[...])
    loads[1].wait()
    snd_kv[:, 0, :, :] = turned(k_in[...])
    loads[2].wait()
    snd_kv[:, 1, :, :] = turned(v_in[...])
    loads[3].wait()
    loads[4].wait()

    pl.semaphore_wait(barrier, (Z - 1) + 3 + (NDP - 1) + 1)

    def cols(j):
        return pl.ds(pl.multiple_of(j * R, R), R)

    def seq_at(ref, p):
        return ref.at[p // 2, p % 2]

    def kv_at(n, g):
        return kvt.at[n, :, :, cols(g)]

    sends = []

    def send(cp):
        cp.start()
        sends.append(cp)

    up, down = (dp, (me + 1) % N), (dp, (me + N - 1) % N)
    send(rcopy(g_in.at[pl.ds(R - 16, 16)], gh.at[0], s_h.at[0], r_h.at[0], up))
    send(rcopy(g_in.at[pl.ds(0, 16)], gh.at[1], s_h.at[1], r_h.at[1], down))

    def send_kv(near):
        for i in zorder:
            p = (z + i) % Z
            n = slot_of[Z - i]
            if (n < 3) == near:
                send(rcopy(snd_kv.at[p], kv_at(n, gm), s_kv.at[i], r_kv.at[n], zpeer(p)))

    send_kv(True)
    for i in zorder:
        p = (z + i) % Z
        send(rcopy(snd_q.at[p], qt.at[:, cols(z)], s_q.at[i], r_q.at[z], zpeer(p)))
    send_kv(False)
    kvt[0, :, :, cols(gm)] = snd_kv[z]

    def grp_copy(n, g, k, to):
        return rcopy(kv_at(n, g), kv_at(n, g), s_grp.at[n, k], r_grp.at[n, g], gpeer(to))

    def share(n):
        grp_copy(n, gm, 1, across).start()
        grp_copy(n, gm, 0, sib).start()

    def relay(n):
        grp_copy(n, across, 1, across).wait_recv()
        grp_copy(n, across, 2, sib).start()

    share(0)
    qt[:, cols(z)] = snd_q[z]

    kgt[...] = jnp.zeros_like(kgt)
    kgt[0:T, :] = ck_in[...]
    for b in range(Z * D // R):
        kg_s1[b * R : (b + 1) * R, :] = kgt[:, b * R : (b + 1) * R].T
    my_taps = kg_s1[pl.ds(pl.multiple_of(z * D, D), D), :]
    for t in range(T):
        kb[t] = jnp.broadcast_to(my_taps[:, t : t + 1], (D, R))
    kga[...] = jnp.zeros_like(kga)
    m_run[...] = jnp.full(m_run.shape, FILL, F32)
    l_run[...] = jnp.zeros_like(l_run)
    acc[...] = jnp.zeros_like(acc)
    dq_acc[...] = jnp.zeros_like(dq_acc)
    gfc[0:D, :] = jnp.zeros((D, NQ), BF16)
    row = lax.broadcasted_iota(jnp.int32, (D, NQ), 0)
    qaug[D : 2 * D, :] = jnp.where(row == 0, 1.0, 0.0).astype(BF16)

    def live_rows(first, count):
        frame = first + lax.broadcasted_iota(jnp.int32, (count, 1), 0)
        return ((frame >= 0) & (frame < length)).astype(F32)

    own_live = live_rows(me * R, R)
    own = g_in[...].astype(F32) * own_live
    gx[16 : 16 + R, :] = own
    snd_g[...] = turned(own)
    rcopy(g_in.at[pl.ds(R - 16, 16)], gh.at[0], s_h.at[0], r_h.at[0], up).wait_recv()
    rcopy(g_in.at[pl.ds(0, 16)], gh.at[1], s_h.at[1], r_h.at[1], down).wait_recv()
    gx[0:16, :] = jnp.where(live_rows(me * R - 16, 16) > 0, gh[0].astype(F32), 0.0)
    gx[16 + R : 32 + R, :] = jnp.where(live_rows(me * R + R, 16) > 0, gh[1].astype(F32), 0.0)

    def grad_block(b, carry):
        at = cols(b)
        total = gx[16 : 16 + R, at]
        for t in range(T):
            total = total + ck_in[t : t + 1, at] * gx[pl.ds(16 + HALF - t, R), at]
        gx2 = (total * own_live).T.astype(BF16)
        for h in range(R // D):
            snd_d[(R // D) * b + h] = gx2[h * D : (h + 1) * D]
        return carry

    lax.fori_loop(0, Z * D // R, grad_block, 0)
    for i in zorder:
        p = (z + i) % Z
        send(rcopy(snd_d.at[p], dot_t.at[:, cols(z)], s_d.at[i], r_d.at[z], zpeer(p)))
    for i in zorder:
        p = (z + i) % Z
        send(rcopy(snd_g.at[p], gbuf.at[z], s_g.at[i], r_g.at[z], zpeer(p)))
    dot_t[:, cols(z)] = snd_d[z]
    gbuf[z] = snd_g[z]

    def halo(seq, n):
        mine = seq.at[pl.ds(c, Z), 1 - c]
        rcopy(mine, mine, s_h.at[n], r_h.at[n], gpeer(gm + 1 - 2 * c)).start()

        @pl.when(x != c)
        def _():
            rcopy(
                seq.at[c * Z, 1 - c], seq.at[(1 - c) * Z, 1 - c],
                s_h.at[n + 1], r_h.at[n + 1], gpeer(3 - gm),
            ).start()

    def halo_wait(seq, n):
        mine = seq.at[pl.ds(c, Z), 1 - c]
        other = seq.at[pl.ds(1 - c, Z), c]
        cp = rcopy(mine, other, s_h.at[n], r_h.at[n], gpeer(gm + 1 - 2 * c))
        cp.wait_send()
        cp.wait_recv()

        @pl.when(x != c)
        def _():
            cp2 = rcopy(
                seq.at[c * Z, 1 - c], seq.at[c * Z, c],
                s_h.at[n + 1], r_h.at[n + 1], gpeer(3 - gm),
            )
            cp2.wait_send()
            cp2.wait_recv()

    lane = lax.broadcasted_iota(jnp.int32, (1, R), 1)

    def live_of(j):
        return ((x * 2 * Z + 2 * j + c) * R + lane < length).astype(F32)

    def window(seq, j):
        p = 1 + 2 * j + c
        parts = [seq[(p + d) // 2, (p + d) % 2].astype(F32) for d in (-1, 0, 1)]
        return jnp.concatenate(parts, axis=1), parts[1]

    def shifted(wide, s):
        if s == 0:
            return wide[:, R : 2 * R]
        return pltpu.roll(wide, (3 * R - s) % (3 * R), 1)[:, R : 2 * R]

    def arrive(n):
        rcopy(kv_at(n, gm), kv_at(n, gm), s_kv.at[0], r_kv.at[n], gpeer(across)).wait_recv()
        share(n)

    arrive(1)
    relay(0)
    if Z > 2:
        arrive(2)
    for i in zorder:
        p = (z + i) % Z
        rcopy(snd_q.at[p], qt.at[:, cols(p)], s_q.at[i], r_q.at[p], zpeer(p)).wait_recv()
    qaug[0:D, :] = (qt[...].astype(F32) * (D ** -0.5)).astype(BF16)

    lane_full = lax.broadcasted_iota(jnp.int32, (R, R), 1)
    sub_full = lax.broadcasted_iota(jnp.int32, (R, R), 0)

    def keys_at(n):
        return pl.ds(pl.multiple_of(n * CK, CK), CK)

    def forward(n, carry):
        @pl.when(n < Z)
        def _():
            arrive(n)

        @pl.when(n - 2 < Z)
        def _():
            relay(n - 2)

        m = n - 3
        zs = (z + off_of(m)) % Z
        grp_copy(m, sib, 0, sib).wait_recv()
        grp_copy(m, across_sib, 2, sib).wait_recv()
        for g in range(4):
            blk = kvt[m, :, :, g * R : (g + 1) * R].reshape(2 * D, R).astype(F32).T
            at = pl.ds(pl.multiple_of(m * CK + g * R, R), R)
            kvn[at, :] = blk.astype(BF16)
            frame = ((g // 2) * 2 * Z + 2 * zs + g % 2) * R + sub_full
            fill = jnp.where((lane_full == D) & (frame >= length), FILL, 0.0)
            kaug[at, :] = jnp.where(lane_full < D, blk, fill).astype(BF16)
        at = keys_at(m)
        s = dot(kaug[at, :], qaug[...])
        m_old = m_run[0:1, :]
        m_new = jnp.maximum(m_old, jnp.max(s, axis=0, keepdims=True))
        w = jnp.exp(s - m_new)
        alpha = jnp.exp(m_old - m_new)
        l_run[0:1, :] = l_run[0:1, :] * alpha + jnp.sum(w, axis=0, keepdims=True)
        wb = w.astype(BF16)
        w_all[at, :] = wb
        acc[...] = acc[...] * alpha + dot(kvt[m, 1], wb)
        m_run[0:1, :] = m_new
        m_all[m, 0:1, :] = m_new
        return carry

    lax.fori_loop(3, Z + 3, forward, 0)

    for i in zorder:
        p = (z + i) % Z
        rcopy(snd_d.at[p], dot_t.at[:, cols(p)], s_d.at[i], r_d.at[p], zpeer(p)).wait_recv()


    inv = 1.0 / l_run[0:1, :]
    l_run[0:1, :] = inv
    att = (acc[...] * inv).astype(BF16)
    for j in range(Z):
        blk = (att[:, j * R : (j + 1) * R].astype(F32) * live_of(j)).astype(BF16)
        oseq[(1 + 2 * j + c) // 2, (1 + 2 * j + c) % 2] = blk
    halo(oseq, 2)
    m_run[1:2, :] = jnp.sum(dot_t[...].astype(F32) * att.astype(F32), axis=0, keepdims=True)

    def out_block(j, carry):
        wide, mid = window(oseq, j)
        grad = gbuf[j].astype(F32)
        total = mid
        for t in range(T):
            seg = shifted(wide, t - HALF)
            total = total + kb[t] * seg
            kga[t] = kga[t] + grad * seg
        mix_s[j] = (total * live_of(j)).astype(BF16)
        return carry

    def mix_copy(i, p, h):
        return rcopy(mix_s.at[p], land.at[h, 0], s_m.at[i], r_m.at[h], zpeer(p))

    def taps_a(i):
        g = (gm + i) % 4
        return rcopy(kg_grp.at[gm], kg_grp.at[gm], s_kg.at[i], r_kg.at[gm], gpeer(g))

    def taps_a_in(i):
        g = (gm + i) % 4
        return rcopy(kg_grp.at[g], kg_grp.at[g], s_kg.at[i], r_kg.at[g], gpeer(g))

    def taps_b(i):
        return rcopy(kg_dp.at[dp], kg_dp.at[dp], s_kg.at[4 + i], r_kg.at[4 + dp], ((dp + i) % NDP, me))

    def taps_b_in(i):
        p = (dp + i) % NDP
        return rcopy(kg_dp.at[p], kg_dp.at[p], s_kg.at[4 + i], r_kg.at[4 + p], (p, me))

    def taps_c(i, p, h):
        return rcopy(kg_s, kg_land.at[h], s_kg.at[4 + NDP + i], r_kg.at[4 + NDP + h], zpeer(p))

    def part_copy(n, i):
        g = (gm + i) % 4
        return rcopy(part.at[n, :, :, cols(g)], gred.at[n, gm], s_p.at[n, i], r_p.at[n, gm], gpeer(g))

    def part_in(n, i):
        g = (gm + i) % 4
        return rcopy(part.at[n, :, :, cols(g)], gred.at[n, g], s_p.at[n, i], r_p.at[n, g], gpeer(g))

    def add_up(n):
        for i in range(1, 4):
            part_in(n, i).wait_recv()
        gred[n, gm] = part[n, :, :, cols(gm)]
        total = (gred[n, 0].astype(F32) + gred[n, 1].astype(F32)) + (
            gred[n, 2].astype(F32) + gred[n, 3].astype(F32)
        )
        kv_s[n] = total.astype(BF16)

    def kv_copy(n, h):
        return rcopy(kv_s.at[n], land.at[h, pl.ds(2, 2)], s_o.at[n], r_o.at[h], zpeer((z + off_of(n)) % Z))

    def backward(k, carry):
        n = Z - 1 - k
        at = keys_at(n)
        f = jnp.exp(m_all[n, 0:1, :] - m_run[0:1, :]) * l_run[0:1, :]
        gf = (dot_t[...].astype(F32) * f).astype(BF16)
        gfc[D : 2 * D, :] = gf
        dp_t = dot(kvn[at, :], gfc[...])
        wb = w_all[at, :]
        ds = (wb.astype(F32) * (dp_t - m_run[1:2, :] * f)).astype(BF16)
        part[n, 0] = (dot(qt[...], ds, NT) * (D ** -0.5)).astype(BF16)
        part[n, 1] = dot(gf, wb, NT).astype(BF16)
        for i in range(1, 4):
            part_copy(n, i).start()
        dq_acc[...] = dq_acc[...] + dot(kvt[n, 0], ds)

        @pl.when(k > 1)
        def _():
            add_up(n + 2)
            kv_copy(n + 2, z).start()

        @pl.when(k == 1)
        def _():
            for i in zorder:
                p = (z + i) % Z
                rcopy(snd_g.at[p], gbuf.at[p], s_g.at[i], r_g.at[p], zpeer(p)).wait_recv()
            halo_wait(oseq, 2)
            lax.fori_loop(0, Z, out_block, 0)
            for i in zorder:
                mix_copy(i, (z + i) % Z, z).start()
            lane_d = lax.broadcasted_iota(jnp.int32, (D, R), 1)
            red = jnp.zeros((D, R), F32)
            for t in range(T):
                red = jnp.where(lane_d == t, jnp.sum(kga[t], axis=1, keepdims=True), red)
            flat = jnp.concatenate([red, jnp.zeros((R - D, R), F32)], axis=0).T
            kg_grp[gm] = jnp.concatenate([flat[0:16, 0:D], flat[16:32, 0:D]], axis=1)
            for i in range(1, 4):
                taps_a(i).start()

        @pl.when(k == min(4, Z - 1))
        def _():
            for i in range(1, 4):
                taps_a_in(i).wait_recv()
            kg_dp[dp] = (kg_grp[0] + kg_grp[1]) + (kg_grp[2] + kg_grp[3])
            for i in range(1, NDP):
                taps_b(i).start()

        return carry

    lax.fori_loop(0, Z, backward, 0)

    for j in range(Z):
        dq_s[j] = (dq_acc[:, j * R : (j + 1) * R] * (D ** -0.5)).astype(BF16)

    def dq_copy(i, p, h):
        return rcopy(dq_s.at[p], land.at[h, 1], s_dq.at[i], r_dq.at[h], zpeer(p))

    for i in zorder:
        dq_copy(i, (z + i) % Z, z).start()
    add_up(1)
    kv_copy(1, z).start()
    for i in range(1, NDP):
        taps_b_in(i).wait_recv()
    total = kg_dp[0]
    for i in range(1, NDP):
        total = total + kg_dp[i]
    kg_s[...] = total
    for i in zorder:
        taps_c(i, (z + i) % Z, z).start()
    add_up(0)
    local = [
        pltpu.make_async_copy(mix_s.at[z], land.at[z, 0], s_loc.at[0]),
        pltpu.make_async_copy(dq_s.at[z], land.at[z, 1], s_loc.at[1]),
        pltpu.make_async_copy(kv_s.at[0], land.at[z, pl.ds(2, 2)], s_loc.at[2]),
        pltpu.make_async_copy(kg_s, kg_land.at[z], s_loc.at[3]),
    ]
    for cp in local:
        cp.start()

    for cp in sends:
        cp.wait_send()

    def drain(n, carry):
        grp_copy(n, gm, 0, sib).wait_send()
        grp_copy(n, gm, 1, across).wait_send()
        grp_copy(n, across, 2, sib).wait_send()
        for i in range(1, 4):
            part_copy(n, i).wait_send()
        return carry

    lax.fori_loop(0, Z, drain, 0)
    for i in range(1, 4):
        taps_a(i).wait_send()
    for i in range(1, NDP):
        taps_b(i).wait_send()
    for i in zorder:
        p = (z + i) % Z
        for cp in (mix_copy(i, p, p), taps_c(i, p, p), dq_copy(i, p, p)):
            cp.wait_send()
            cp.wait_recv()
        kv_copy(slot_of[i], p).wait_send()
        kv_copy(slot_of[i], p).wait_recv()
    for cp in local:
        cp.wait()


def finish(Z, T, land, kg, mix_out, dq_out, dk_out, dv_out, kg_out):
    for n, out in enumerate((mix_out, dq_out, dk_out, dv_out)):
        out[...] = land[:, n].astype(F32).reshape(Z * D, R).T.astype(BF16)
    def taps_of(h):
        return jnp.concatenate([kg[h][:, 0:D], kg[h][:, D : 2 * D]], axis=0)[0:T]

    for h in range(0, Z, 2):
        kg_out[:, h * D : (h + 2) * D] = jnp.concatenate([taps_of(h), taps_of(h + 1)], axis=1)


def per_device(Z, NDP, lengths, q, k, v, g, taps):
    W = Z * D
    NQ = R * Z
    NK = 4 * NQ
    T = taps.shape[0]
    CK = 4 * R
    vm = pltpu.VMEM
    dma = pltpu.SemaphoreType.DMA
    scratch = [
        vm((R, W), BF16), vm((R, W), BF16), vm((R, W), BF16), vm((R, W), BF16), vm((T, W), F32),
        vm((Z, 2, D, R), BF16), vm((Z, D, R), BF16), vm((Z, D, R), BF16), vm((Z, D, R), BF16),
        vm((R + 32, W), F32), vm((2, 16, W), BF16), vm((Z, D, R), BF16),
        vm((Z, 2, D, CK), BF16), vm((NK, 2 * D), BF16), vm((NK, 2 * D), BF16),
        vm((D, NQ), BF16), vm((2 * D, NQ), BF16),
        vm((Z + 1, 2, D, R), BF16),
        vm((D, NQ), BF16), vm((2 * D, NQ), BF16),
        vm((T, D, R), F32), vm((T, D, R), F32), vm((R, W), F32),
        vm((4, 16, R), F32), vm((NDP, 16, R), F32), vm((16, R), F32), vm((W, R), F32),
        vm((NK, NQ), BF16), vm((Z, 8, NQ), F32), vm((8, NQ), F32), vm((8, NQ), F32),
        vm((D, NQ), F32), vm((D, NQ), F32),
        vm((Z, D, R), BF16), vm((Z, D, R), BF16),
        vm((Z, 2, D, CK), BF16), vm((Z, 4, 2, D, R), BF16), vm((Z, 2, D, R), BF16),
        dma((5,)),
        dma((Z,)), dma((Z,)), dma((Z,)), dma((Z,)), dma((Z,)), dma((Z,)), dma((Z,)), dma((Z,)),
        dma((Z, 4)), dma((Z, 4)), dma((4,)), dma((4,)),
        dma((4 + NDP + Z,)), dma((4 + NDP + Z,)), dma((Z,)), dma((Z,)), dma((Z,)), dma((Z,)),
        dma((Z, 4)), dma((Z, 4)), dma((Z,)), dma((Z,)), dma((4,)),
    ]
    vspec = pl.BlockSpec(memory_space=pltpu.VMEM)
    anyspec = pl.BlockSpec(memory_space=pl.ANY)
    land, kg = pl.pallas_call(
        functools.partial(kernel, Z, NDP),
        out_shape=(
            jax.ShapeDtypeStruct((Z, 4, D, R), BF16),
            jax.ShapeDtypeStruct((Z, 16, R), F32),
        ),
        in_specs=[pl.BlockSpec(memory_space=pltpu.SMEM)] + [anyspec] * 5,
        out_specs=(anyspec, anyspec),
        scratch_shapes=scratch,
        compiler_params=pltpu.CompilerParams(
            collective_id=0, has_side_effects=True, vmem_limit_bytes=56 * 1024 * 1024
        ),
        cost_estimate=pl.CostEstimate(
            flops=12 * NQ * NK * D, bytes_accessed=9 * R * W * 2, transcendentals=NQ * NK
        ),
    )(lengths, q[0], k[0], v[0], g[0], taps)
    outs = pl.pallas_call(
        functools.partial(finish, Z, T),
        out_shape=(
            jax.ShapeDtypeStruct((R, W), BF16), jax.ShapeDtypeStruct((R, W), BF16),
            jax.ShapeDtypeStruct((R, W), BF16), jax.ShapeDtypeStruct((R, W), BF16),
            jax.ShapeDtypeStruct((T, W), F32),
        ),
        in_specs=[vspec] * 2,
        out_specs=(vspec,) * 5,
    )(land, kg)
    return outs[0][None], outs[1][None], outs[2][None], outs[3][None], outs[4]


def solution(mesh):
    Z = mesh.shape["ctx"] // 4
    NDP = mesh.shape["dp"]
    split = P("dp", "ctx", None)
    return jax.shard_map(
        functools.partial(per_device, Z, NDP),
        mesh=mesh,
        in_specs=(P(), split, split, split, split, P()),
        out_specs=(split, split, split, split, P()),
        check_vma=False,
    )
```

```python
import functools

import jax
import jax.numpy as jnp
from jax import lax
from jax.experimental import pallas as pl
from jax.experimental.pallas import tpu as pltpu
from jax.sharding import PartitionSpec as P

MESH = pl.DeviceIdType.MESH
D = 64
R = 128
FILL = -1e30
F32 = jnp.float32
BF16 = jnp.bfloat16

NN = (((1,), (0,)), ((), ()))
NT = (((1,), (1,)), ((), ()))


def dot(a, b, dims=NN):
    return lax.dot_general(a, b, dims, preferred_element_type=F32)


def kernel(
    Z, NDP,
    len_ref, q_hbm, k_hbm, v_hbm, g_hbm, ck_hbm,
    land, kg_land,
    q_in, k_in, v_in, g_in, ck_in,
    snd_kv, snd_q, snd_g, snd_d, gx, gh, gbuf, kvt, kvn, kaug, qt, qaug, oseq, dot_t, gfc,
    kb, kga, kgt, ox, kg_grp, kg_dp, kg_s,
    w_all, m_all, m_run, l_run, acc, dq_acc, mix_s, dq_s, part, gred, kv_s,
    s_in, s_kv, r_kv, s_q, r_q, s_g, r_g, s_d, r_d, s_grp, r_grp, s_h, r_h,
    s_kg, r_kg, s_m, r_m, s_dq, r_dq, s_p, r_p, s_o, r_o, s_loc,
):
    NQ = R * Z
    CK = 4 * R
    T = ck_in.shape[0]
    HALF = (T - 1) // 2
    me = lax.axis_index("ctx")
    dp = lax.axis_index("dp")
    x = me // (2 * Z)
    z = (me // 2) % Z
    c = me % 2
    gm = 2 * x + c
    N = 4 * Z
    sib = gm + 1 - 2 * c
    across = (gm + 2) % 4
    across_sib = 3 - gm
    length = len_ref[dp]

    def zpeer(p):
        return (dp, x * 2 * Z + 2 * p + c)

    def gpeer(g):
        return (dp, (g // 2) * 2 * Z + 2 * z + g % 2)

    def rcopy(src, dst, ssem, rsem, dev):
        return pltpu.make_async_remote_copy(
            src_ref=src, dst_ref=dst, send_sem=ssem, recv_sem=rsem, device_id=dev, device_id_type=MESH
        )

    offs = [0]
    for i in range(1, Z // 2 + 1):
        offs.append(i)
        if Z - i != i:
            offs.append(Z - i)
    zorder = offs[1:]
    slot_of = {o: n for n, o in enumerate(offs)}

    def off_of(n):
        odd = n % 2
        return odd * ((n + 1) // 2) + (1 - odd) * ((Z - n // 2) % Z)

    zero_blk = jnp.zeros((D, R), BF16)
    oseq[0, 0] = zero_blk
    oseq[Z, 1] = zero_blk

    barrier = pltpu.get_barrier_semaphore()
    for i in range(1, Z):
        pl.semaphore_signal(barrier, inc=1, device_id=zpeer((z + i) % Z), device_id_type=MESH)
    for i in range(1, 4):
        pl.semaphore_signal(barrier, inc=1, device_id=gpeer((gm + i) % 4), device_id_type=MESH)
    for i in range(1, NDP):
        pl.semaphore_signal(barrier, inc=1, device_id=((dp + i) % NDP, me), device_id_type=MESH)
    pl.semaphore_signal(barrier, inc=1, device_id=(dp, (me + 2 * c - 1 + N) % N), device_id_type=MESH)

    loads = []
    for n, (a, b) in enumerate(((q_hbm, q_in), (k_hbm, k_in), (v_hbm, v_in), (g_hbm, g_in), (ck_hbm, ck_in))):
        cp = pltpu.make_async_copy(a, b, s_in.at[n])
        cp.start()
        loads.append(cp)

    turned = lambda a: a.astype(F32).T.astype(BF16).reshape(Z, D, R)
    loads[0].wait()
    snd_q[...] = turned(q_in[...])
    loads[1].wait()
    snd_kv[:, 0, :, :] = turned(k_in[...])
    loads[2].wait()
    snd_kv[:, 1, :, :] = turned(v_in[...])
    loads[3].wait()
    loads[4].wait()

    pl.semaphore_wait(barrier, (Z - 1) + 3 + (NDP - 1) + 1)

    def cols(j):
        return pl.ds(pl.multiple_of(j * R, R), R)

    def seq_at(ref, p):
        return ref.at[p // 2, p % 2]

    def kv_at(n, g):
        return kvt.at[n, :, :, cols(g)]

    sends = []

    def send(cp):
        cp.start()
        sends.append(cp)

    up, down = (dp, (me + 1) % N), (dp, (me + N - 1) % N)
    send(rcopy(g_in.at[pl.ds(R - 16, 16)], gh.at[0], s_h.at[0], r_h.at[0], up))
    send(rcopy(g_in.at[pl.ds(0, 16)], gh.at[1], s_h.at[1], r_h.at[1], down))

    def send_kv(near):
        for i in zorder:
            p = (z + i) % Z
            n = slot_of[Z - i]
            if (n < 3) == near:
                send(rcopy(snd_kv.at[p], kv_at(n, gm), s_kv.at[i], r_kv.at[n], zpeer(p)))

    send_kv(True)
    for i in zorder:
        p = (z + i) % Z
        send(rcopy(snd_q.at[p], qt.at[:, cols(z)], s_q.at[i], r_q.at[z], zpeer(p)))
    send_kv(False)
    kvt[0, :, :, cols(gm)] = snd_kv[z]

    def grp_copy(n, g, k, to):
        return rcopy(kv_at(n, g), kv_at(n, g), s_grp.at[n, k], r_grp.at[n, g], gpeer(to))

    def share(n):
        grp_copy(n, gm, 1, across).start()
        grp_copy(n, gm, 0, sib).start()

    def relay(n):
        grp_copy(n, across, 1, across).wait_recv()
        grp_copy(n, across, 2, sib).start()

    share(0)
    qt[:, cols(z)] = snd_q[z]

    pair = ck_in[:, cols(z // 2)]
    swapped = pltpu.roll(pair, D, 1)
    in_low = lax.broadcasted_iota(jnp.int32, (T, R), 1) // D
    kb[...] = jnp.where(in_low == z % 2, pair, swapped)
    kga[...] = jnp.zeros_like(kga)
    m_run[...] = jnp.full(m_run.shape, FILL, F32)
    l_run[...] = jnp.zeros_like(l_run)
    acc[...] = jnp.zeros_like(acc)
    dq_acc[...] = jnp.zeros_like(dq_acc)
    gfc[0:D, :] = jnp.zeros((D, NQ), BF16)
    row = lax.broadcasted_iota(jnp.int32, (D, NQ), 0)
    qaug[D : 2 * D, :] = jnp.where(row == 0, 1.0, 0.0).astype(BF16)

    def live_rows(first, count):
        frame = first + lax.broadcasted_iota(jnp.int32, (count, 1), 0)
        return ((frame >= 0) & (frame < length)).astype(F32)

    own_live = live_rows(me * R, R)
    own = g_in[...].astype(F32) * own_live
    gx[16 : 16 + R, :] = own
    snd_g[...] = turned(own)
    rcopy(g_in.at[pl.ds(R - 16, 16)], gh.at[0], s_h.at[0], r_h.at[0], up).wait_recv()
    rcopy(g_in.at[pl.ds(0, 16)], gh.at[1], s_h.at[1], r_h.at[1], down).wait_recv()
    gx[0:16, :] = jnp.where(live_rows(me * R - 16, 16) > 0, gh[0].astype(F32), 0.0)
    gx[16 + R : 32 + R, :] = jnp.where(live_rows(me * R + R, 16) > 0, gh[1].astype(F32), 0.0)

    def grad_block(b, carry):
        at = cols(b)
        total = gx[16 : 16 + R, at]
        for t in range(T):
            total = total + ck_in[t : t + 1, at] * gx[pl.ds(16 + HALF - t, R), at]
        gx2 = (total * own_live).T.astype(BF16)
        for h in range(R // D):
            snd_d[(R // D) * b + h] = gx2[h * D : (h + 1) * D]
        return carry

    lax.fori_loop(0, Z * D // R, grad_block, 0)
    for i in zorder:
        p = (z + i) % Z
        send(rcopy(snd_d.at[p], dot_t.at[:, cols(z)], s_d.at[i], r_d.at[z], zpeer(p)))
    for i in zorder:
        p = (z + i) % Z
        send(rcopy(snd_g.at[p], gbuf.at[z], s_g.at[i], r_g.at[z], zpeer(p)))
    dot_t[:, cols(z)] = snd_d[z]
    gbuf[z] = snd_g[z]

    def halo(seq, n):
        mine = seq.at[pl.ds(c, Z), 1 - c]
        rcopy(mine, mine, s_h.at[n], r_h.at[n], gpeer(gm + 1 - 2 * c)).start()

        @pl.when(x != c)
        def _():
            rcopy(
                seq.at[c * Z, 1 - c], seq.at[(1 - c) * Z, 1 - c],
                s_h.at[n + 1], r_h.at[n + 1], gpeer(3 - gm),
            ).start()

    def halo_wait(seq, n):
        mine = seq.at[pl.ds(c, Z), 1 - c]
        other = seq.at[pl.ds(1 - c, Z), c]
        cp = rcopy(mine, other, s_h.at[n], r_h.at[n], gpeer(gm + 1 - 2 * c))
        cp.wait_send()
        cp.wait_recv()

        @pl.when(x != c)
        def _():
            cp2 = rcopy(
                seq.at[c * Z, 1 - c], seq.at[c * Z, c],
                s_h.at[n + 1], r_h.at[n + 1], gpeer(3 - gm),
            )
            cp2.wait_send()
            cp2.wait_recv()

    lane = lax.broadcasted_iota(jnp.int32, (1, R), 1)

    def live_of(j):
        return ((x * 2 * Z + 2 * j + c) * R + lane < length).astype(F32)

    def window(seq, j):
        p = 1 + 2 * j + c
        parts = [seq[(p + d) // 2, (p + d) % 2].astype(F32) for d in (-1, 0, 1)]
        return parts

    def arrive(n):
        rcopy(kv_at(n, gm), kv_at(n, gm), s_kv.at[0], r_kv.at[n], gpeer(across)).wait_recv()
        share(n)

    arrive(1)
    relay(0)
    if Z > 2:
        arrive(2)
    for i in zorder:
        p = (z + i) % Z
        rcopy(snd_q.at[p], qt.at[:, cols(p)], s_q.at[i], r_q.at[p], zpeer(p)).wait_recv()
    qaug[0:D, :] = (qt[...].astype(F32) * (D ** -0.5)).astype(BF16)

    lane_full = lax.broadcasted_iota(jnp.int32, (R, R), 1)
    sub_full = lax.broadcasted_iota(jnp.int32, (R, R), 0)

    def keys_at(n):
        return pl.ds(pl.multiple_of(n * CK, CK), CK)

    def forward(n, carry):
        @pl.when(n < Z)
        def _():
            arrive(n)

        @pl.when(n - 2 < Z)
        def _():
            relay(n - 2)

        m = n - 3
        zs = (z + off_of(m)) % Z
        grp_copy(m, sib, 0, sib).wait_recv()
        grp_copy(m, across_sib, 2, sib).wait_recv()
        for g in range(4):
            blk = kvt[m, :, :, g * R : (g + 1) * R].reshape(2 * D, R).astype(F32).T
            at = pl.ds(pl.multiple_of(m * CK + g * R, R), R)
            kvn[at, :] = blk.astype(BF16)
            frame = ((g // 2) * 2 * Z + 2 * zs + g % 2) * R + sub_full
            fill = jnp.where((lane_full == D) & (frame >= length), FILL, 0.0)
            kaug[at, :] = jnp.where(lane_full < D, blk, fill).astype(BF16)
        at = keys_at(m)
        s = dot(kaug[at, :], qaug[...])
        m_old = m_run[0:1, :]
        m_new = jnp.maximum(m_old, jnp.max(s, axis=0, keepdims=True))
        w = jnp.exp(s - m_new)
        alpha = jnp.exp(m_old - m_new)
        l_run[0:1, :] = l_run[0:1, :] * alpha + jnp.sum(w, axis=0, keepdims=True)
        wb = w.astype(BF16)
        w_all[at, :] = wb
        acc[...] = acc[...] * alpha + dot(kvt[m, 1], wb)
        m_run[0:1, :] = m_new
        m_all[m, 0:1, :] = m_new
        return carry

    lax.fori_loop(3, Z + 3, forward, 0)

    for i in zorder:
        p = (z + i) % Z
        rcopy(snd_d.at[p], dot_t.at[:, cols(p)], s_d.at[i], r_d.at[p], zpeer(p)).wait_recv()


    inv = 1.0 / l_run[0:1, :]
    l_run[0:1, :] = inv
    att = (acc[...] * inv).astype(BF16)
    for j in range(Z):
        blk = (att[:, j * R : (j + 1) * R].astype(F32) * live_of(j)).astype(BF16)
        oseq[(1 + 2 * j + c) // 2, (1 + 2 * j + c) % 2] = blk
    halo(oseq, 2)
    m_run[1:2, :] = jnp.sum(dot_t[...].astype(F32) * att.astype(F32), axis=0, keepdims=True)

    HZ = Z // 2

    def out_block(j, carry):
        low, high = window(oseq, j), window(oseq, j + HZ)
        for n in range(3):
            ox[n * R : (n + 1) * R, :] = jnp.concatenate([low[n], high[n]], axis=0).T
        grad = jnp.concatenate([gbuf[j].astype(F32), gbuf[j + HZ].astype(F32)], axis=0).T
        total = ox[R : 2 * R, :]
        for t in range(T):
            seg = ox[pl.ds(R + t - HALF, R), :]
            total = total + kb[t : t + 1, :] * seg
            kga[t] = kga[t] + jnp.sum((grad * seg).reshape(R // 8, 8, R), axis=0)
        mixed = total.T
        mix_s[j] = (mixed[0:D] * live_of(j)).astype(BF16)
        mix_s[j + HZ] = (mixed[D : 2 * D] * live_of(j + HZ)).astype(BF16)
        return carry

    def mix_copy(i, p, h):
        return rcopy(mix_s.at[p], land.at[h, 0], s_m.at[i], r_m.at[h], zpeer(p))

    def taps_a(i):
        g = (gm + i) % 4
        return rcopy(kg_grp.at[gm], kg_grp.at[gm], s_kg.at[i], r_kg.at[gm], gpeer(g))

    def taps_a_in(i):
        g = (gm + i) % 4
        return rcopy(kg_grp.at[g], kg_grp.at[g], s_kg.at[i], r_kg.at[g], gpeer(g))

    def taps_b(i):
        return rcopy(kg_dp.at[dp], kg_dp.at[dp], s_kg.at[4 + i], r_kg.at[4 + dp], ((dp + i) % NDP, me))

    def taps_b_in(i):
        p = (dp + i) % NDP
        return rcopy(kg_dp.at[p], kg_dp.at[p], s_kg.at[4 + i], r_kg.at[4 + p], (p, me))

    def taps_c(i, p, h):
        return rcopy(kg_s, kg_land.at[h], s_kg.at[4 + NDP + i], r_kg.at[4 + NDP + h], zpeer(p))

    def part_copy(n, i):
        g = (gm + i) % 4
        return rcopy(part.at[n, :, :, cols(g)], gred.at[n, gm], s_p.at[n, i], r_p.at[n, gm], gpeer(g))

    def part_in(n, i):
        g = (gm + i) % 4
        return rcopy(part.at[n, :, :, cols(g)], gred.at[n, g], s_p.at[n, i], r_p.at[n, g], gpeer(g))

    def add_up(n):
        for i in range(1, 4):
            part_in(n, i).wait_recv()
        gred[n, gm] = part[n, :, :, cols(gm)]
        total = (gred[n, 0].astype(F32) + gred[n, 1].astype(F32)) + (
            gred[n, 2].astype(F32) + gred[n, 3].astype(F32)
        )
        kv_s[n] = total.astype(BF16)

    def kv_copy(n, h):
        return rcopy(kv_s.at[n], land.at[h, pl.ds(2, 2)], s_o.at[n], r_o.at[h], zpeer((z + off_of(n)) % Z))

    def backward(k, carry):
        n = Z - 1 - k
        at = keys_at(n)
        f = jnp.exp(m_all[n, 0:1, :] - m_run[0:1, :]) * l_run[0:1, :]
        gf = (dot_t[...].astype(F32) * f).astype(BF16)
        gfc[D : 2 * D, :] = gf
        dp_t = dot(kvn[at, :], gfc[...])
        wb = w_all[at, :]
        ds = (wb.astype(F32) * (dp_t - m_run[1:2, :] * f)).astype(BF16)
        part[n, 0] = (dot(qt[...], ds, NT) * (D ** -0.5)).astype(BF16)
        part[n, 1] = dot(gf, wb, NT).astype(BF16)
        for i in range(1, 4):
            part_copy(n, i).start()
        dq_acc[...] = dq_acc[...] + dot(kvt[n, 0], ds)

        @pl.when(k > 1)
        def _():
            add_up(n + 2)
            kv_copy(n + 2, z).start()

        @pl.when(k == 1)
        def _():
            for i in zorder:
                p = (z + i) % Z
                rcopy(snd_g.at[p], gbuf.at[p], s_g.at[i], r_g.at[p], zpeer(p)).wait_recv()
            halo_wait(oseq, 2)
            lax.fori_loop(0, HZ, out_block, 0)
            for i in zorder:
                mix_copy(i, (z + i) % Z, z).start()
            kgt[...] = jnp.zeros_like(kgt)
            for t in range(T):
                kgt[t : t + 1, :] = jnp.sum(kga[t], axis=0, keepdims=True)
            rows = kgt[...]
            rows = rows + pltpu.roll(rows, D, 1)
            low_half = lax.broadcasted_iota(jnp.int32, (16, R), 1) < D
            kg_grp[gm] = jnp.where(low_half, rows[0:16], rows[16:32])
            for i in range(1, 4):
                taps_a(i).start()

        @pl.when(k == min(4, Z - 1))
        def _():
            for i in range(1, 4):
                taps_a_in(i).wait_recv()
            kg_dp[dp] = (kg_grp[0] + kg_grp[1]) + (kg_grp[2] + kg_grp[3])
            for i in range(1, NDP):
                taps_b(i).start()

        return carry

    lax.fori_loop(0, Z, backward, 0)

    for j in range(Z):
        dq_s[j] = (dq_acc[:, j * R : (j + 1) * R] * (D ** -0.5)).astype(BF16)

    def dq_copy(i, p, h):
        return rcopy(dq_s.at[p], land.at[h, 1], s_dq.at[i], r_dq.at[h], zpeer(p))

    for i in zorder:
        dq_copy(i, (z + i) % Z, z).start()
    add_up(1)
    kv_copy(1, z).start()
    for i in range(1, NDP):
        taps_b_in(i).wait_recv()
    total = kg_dp[0]
    for i in range(1, NDP):
        total = total + kg_dp[i]
    kg_s[...] = total
    for i in zorder:
        taps_c(i, (z + i) % Z, z).start()
    add_up(0)
    local = [
        pltpu.make_async_copy(mix_s.at[z], land.at[z, 0], s_loc.at[0]),
        pltpu.make_async_copy(dq_s.at[z], land.at[z, 1], s_loc.at[1]),
        pltpu.make_async_copy(kv_s.at[0], land.at[z, pl.ds(2, 2)], s_loc.at[2]),
        pltpu.make_async_copy(kg_s, kg_land.at[z], s_loc.at[3]),
    ]
    for cp in local:
        cp.start()

    for cp in sends:
        cp.wait_send()

    def drain(n, carry):
        grp_copy(n, gm, 0, sib).wait_send()
        grp_copy(n, gm, 1, across).wait_send()
        grp_copy(n, across, 2, sib).wait_send()
        for i in range(1, 4):
            part_copy(n, i).wait_send()
        return carry

    lax.fori_loop(0, Z, drain, 0)
    for i in range(1, 4):
        taps_a(i).wait_send()
    for i in range(1, NDP):
        taps_b(i).wait_send()
    for i in zorder:
        p = (z + i) % Z
        for cp in (mix_copy(i, p, p), taps_c(i, p, p), dq_copy(i, p, p)):
            cp.wait_send()
            cp.wait_recv()
        kv_copy(slot_of[i], p).wait_send()
        kv_copy(slot_of[i], p).wait_recv()
    for cp in local:
        cp.wait()


def finish(Z, T, land, kg, mix_out, dq_out, dk_out, dv_out, kg_out):
    for n, out in enumerate((mix_out, dq_out, dk_out, dv_out)):
        out[...] = land[:, n].astype(F32).reshape(Z * D, R).T.astype(BF16)
    def taps_of(h):
        return jnp.concatenate([kg[h][:, 0:D], kg[h][:, D : 2 * D]], axis=0)[0:T]

    for h in range(0, Z, 2):
        kg_out[:, h * D : (h + 2) * D] = jnp.concatenate([taps_of(h), taps_of(h + 1)], axis=1)


def per_device(Z, NDP, lengths, q, k, v, g, taps):
    W = Z * D
    NQ = R * Z
    NK = 4 * NQ
    T = taps.shape[0]
    CK = 4 * R
    vm = pltpu.VMEM
    dma = pltpu.SemaphoreType.DMA
    scratch = [
        vm((R, W), BF16), vm((R, W), BF16), vm((R, W), BF16), vm((R, W), BF16), vm((T, W), F32),
        vm((Z, 2, D, R), BF16), vm((Z, D, R), BF16), vm((Z, D, R), BF16), vm((Z, D, R), BF16),
        vm((R + 32, W), F32), vm((2, 16, W), BF16), vm((Z, D, R), BF16),
        vm((Z, 2, D, CK), BF16), vm((NK, 2 * D), BF16), vm((NK, 2 * D), BF16),
        vm((D, NQ), BF16), vm((2 * D, NQ), BF16),
        vm((Z + 1, 2, D, R), BF16),
        vm((D, NQ), BF16), vm((2 * D, NQ), BF16),
        vm((T, R), F32), vm((T, 8, R), F32), vm((32, R), F32), vm((3 * R, R), F32),
        vm((4, 16, R), F32), vm((NDP, 16, R), F32), vm((16, R), F32),
        vm((NK, NQ), BF16), vm((Z, 8, NQ), F32), vm((8, NQ), F32), vm((8, NQ), F32),
        vm((D, NQ), F32), vm((D, NQ), F32),
        vm((Z, D, R), BF16), vm((Z, D, R), BF16),
        vm((Z, 2, D, CK), BF16), vm((Z, 4, 2, D, R), BF16), vm((Z, 2, D, R), BF16),
        dma((5,)),
        dma((Z,)), dma((Z,)), dma((Z,)), dma((Z,)), dma((Z,)), dma((Z,)), dma((Z,)), dma((Z,)),
        dma((Z, 4)), dma((Z, 4)), dma((4,)), dma((4,)),
        dma((4 + NDP + Z,)), dma((4 + NDP + Z,)), dma((Z,)), dma((Z,)), dma((Z,)), dma((Z,)),
        dma((Z, 4)), dma((Z, 4)), dma((Z,)), dma((Z,)), dma((4,)),
    ]
    vspec = pl.BlockSpec(memory_space=pltpu.VMEM)
    anyspec = pl.BlockSpec(memory_space=pl.ANY)
    land, kg = pl.pallas_call(
        functools.partial(kernel, Z, NDP),
        out_shape=(
            jax.ShapeDtypeStruct((Z, 4, D, R), BF16),
            jax.ShapeDtypeStruct((Z, 16, R), F32),
        ),
        in_specs=[pl.BlockSpec(memory_space=pltpu.SMEM)] + [anyspec] * 5,
        out_specs=(anyspec, anyspec),
        scratch_shapes=scratch,
        compiler_params=pltpu.CompilerParams(
            collective_id=0, has_side_effects=True, vmem_limit_bytes=56 * 1024 * 1024
        ),
        cost_estimate=pl.CostEstimate(
            flops=12 * NQ * NK * D, bytes_accessed=9 * R * W * 2, transcendentals=NQ * NK
        ),
    )(lengths, q[0], k[0], v[0], g[0], taps)
    outs = pl.pallas_call(
        functools.partial(finish, Z, T),
        out_shape=(
            jax.ShapeDtypeStruct((R, W), BF16), jax.ShapeDtypeStruct((R, W), BF16),
            jax.ShapeDtypeStruct((R, W), BF16), jax.ShapeDtypeStruct((R, W), BF16),
            jax.ShapeDtypeStruct((T, W), F32),
        ),
        in_specs=[vspec] * 2,
        out_specs=(vspec,) * 5,
    )(land, kg)
    return outs[0][None], outs[1][None], outs[2][None], outs[3][None], outs[4]


def solution(mesh):
    Z = mesh.shape["ctx"] // 4
    NDP = mesh.shape["dp"]
    split = P("dp", "ctx", None)
    return jax.shard_map(
        functools.partial(per_device, Z, NDP),
        mesh=mesh,
        in_specs=(P(), split, split, split, split, P()),
        out_specs=(split, split, split, split, P()),
        check_vma=False,
    )
```

```python
import functools

import jax
import jax.numpy as jnp
from jax import lax
from jax.experimental import pallas as pl
from jax.experimental.pallas import tpu as pltpu
from jax.sharding import PartitionSpec as P

MESH = pl.DeviceIdType.MESH
D = 64
R = 128
FILL = -1e30
F32 = jnp.float32
BF16 = jnp.bfloat16

NN = (((1,), (0,)), ((), ()))
NT = (((1,), (1,)), ((), ()))


def dot(a, b, dims=NN):
    return lax.dot_general(a, b, dims, preferred_element_type=F32)


def kernel(
    Z, NDP,
    len_ref, q_hbm, k_hbm, v_hbm, g_hbm, ck_hbm,
    land, kg_land,
    q_in, k_in, v_in, g_in, ck_in,
    snd_kv, snd_q, snd_g, snd_d, gx, gh, gbuf, kvt, kvn, kaug, qt, qaug, oseq, dot_t, gfc,
    kb, kga, kgt, ox, kg_grp, kg_dp, kg_s,
    w_all, m_all, m_run, l_run, acc, dq_acc, mix_s, dq_s, part, gred, kv_s,
    s_in, s_kv, r_kv, s_q, r_q, s_g, r_g, s_d, r_d, s_grp, r_grp, s_h, r_h,
    s_kg, r_kg, s_m, r_m, s_dq, r_dq, s_p, r_p, s_o, r_o, s_loc,
):
    NQ = R * Z
    CK = 4 * R
    T = ck_in.shape[0]
    HALF = (T - 1) // 2
    me = lax.axis_index("ctx")
    dp = lax.axis_index("dp")
    x = me // (2 * Z)
    z = (me // 2) % Z
    c = me % 2
    gm = 2 * x + c
    N = 4 * Z
    sib = gm + 1 - 2 * c
    across = (gm + 2) % 4
    across_sib = 3 - gm
    length = len_ref[dp]

    def zpeer(p):
        return (dp, x * 2 * Z + 2 * p + c)

    def gpeer(g):
        return (dp, (g // 2) * 2 * Z + 2 * z + g % 2)

    def rcopy(src, dst, ssem, rsem, dev):
        return pltpu.make_async_remote_copy(
            src_ref=src, dst_ref=dst, send_sem=ssem, recv_sem=rsem, device_id=dev, device_id_type=MESH
        )

    offs = [0]
    for i in range(1, Z // 2 + 1):
        offs.append(i)
        if Z - i != i:
            offs.append(Z - i)
    zorder = offs[1:]
    slot_of = {o: n for n, o in enumerate(offs)}

    def off_of(n):
        odd = n % 2
        return odd * ((n + 1) // 2) + (1 - odd) * ((Z - n // 2) % Z)

    zero_blk = jnp.zeros((D, R), BF16)
    oseq[0, 0] = zero_blk
    oseq[Z, 1] = zero_blk

    barrier = pltpu.get_barrier_semaphore()
    for i in range(1, Z):
        pl.semaphore_signal(barrier, inc=1, device_id=zpeer((z + i) % Z), device_id_type=MESH)
    for i in range(1, 4):
        pl.semaphore_signal(barrier, inc=1, device_id=gpeer((gm + i) % 4), device_id_type=MESH)
    for i in range(1, NDP):
        pl.semaphore_signal(barrier, inc=1, device_id=((dp + i) % NDP, me), device_id_type=MESH)
    pl.semaphore_signal(barrier, inc=1, device_id=(dp, (me + 2 * c - 1 + N) % N), device_id_type=MESH)

    loads = []
    for n, (a, b) in enumerate(((q_hbm, q_in), (k_hbm, k_in), (v_hbm, v_in), (g_hbm, g_in), (ck_hbm, ck_in))):
        cp = pltpu.make_async_copy(a, b, s_in.at[n])
        cp.start()
        loads.append(cp)

    turned = lambda a: a.astype(F32).T.astype(BF16).reshape(Z, D, R)
    loads[0].wait()
    snd_q[...] = turned(q_in[...])
    loads[1].wait()
    snd_kv[:, 0, :, :] = turned(k_in[...])
    loads[2].wait()
    snd_kv[:, 1, :, :] = turned(v_in[...])
    loads[3].wait()
    loads[4].wait()

    pl.semaphore_wait(barrier, (Z - 1) + 3 + (NDP - 1) + 1)

    def cols(j):
        return pl.ds(pl.multiple_of(j * R, R), R)

    def seq_at(ref, p):
        return ref.at[p // 2, p % 2]

    def kv_at(n, g):
        return kvt.at[n, :, :, cols(g)]

    sends = []

    def send(cp):
        cp.start()
        sends.append(cp)

    up, down = (dp, (me + 1) % N), (dp, (me + N - 1) % N)
    send(rcopy(g_in.at[pl.ds(R - 16, 16)], gh.at[0], s_h.at[0], r_h.at[0], up))
    send(rcopy(g_in.at[pl.ds(0, 16)], gh.at[1], s_h.at[1], r_h.at[1], down))

    def send_kv(near):
        for i in zorder:
            p = (z + i) % Z
            n = slot_of[Z - i]
            if (n < 3) == near:
                send(rcopy(snd_kv.at[p], kv_at(n, gm), s_kv.at[i], r_kv.at[n], zpeer(p)))

    send_kv(True)
    for i in zorder:
        p = (z + i) % Z
        send(rcopy(snd_q.at[p], qt.at[:, cols(z)], s_q.at[i], r_q.at[z], zpeer(p)))
    send_kv(False)
    kvt[0, :, :, cols(gm)] = snd_kv[z]

    def grp_copy(n, g, k, to):
        return rcopy(kv_at(n, g), kv_at(n, g), s_grp.at[n, k], r_grp.at[n, g], gpeer(to))

    def share(n):
        grp_copy(n, gm, 1, across).start()
        grp_copy(n, gm, 0, sib).start()

    def relay(n):
        grp_copy(n, across, 1, across).wait_recv()
        grp_copy(n, across, 2, sib).start()

    share(0)
    qt[:, cols(z)] = snd_q[z]

    pair = ck_in[:, cols(z // 2)]
    swapped = pltpu.roll(pair, D, 1)
    in_low = lax.broadcasted_iota(jnp.int32, (T, R), 1) // D
    kb[...] = jnp.where(in_low == z % 2, pair, swapped)
    kga[...] = jnp.zeros_like(kga)
    m_run[...] = jnp.full(m_run.shape, FILL, F32)
    l_run[...] = jnp.zeros_like(l_run)
    acc[...] = jnp.zeros_like(acc)
    dq_acc[...] = jnp.zeros_like(dq_acc)
    gfc[0:D, :] = jnp.zeros((D, NQ), BF16)
    row = lax.broadcasted_iota(jnp.int32, (D, NQ), 0)
    qaug[D : 2 * D, :] = jnp.where(row == 0, 1.0, 0.0).astype(BF16)

    def live_rows(first, count):
        frame = first + lax.broadcasted_iota(jnp.int32, (count, 1), 0)
        return ((frame >= 0) & (frame < length)).astype(F32)

    own_live = live_rows(me * R, R)
    own = g_in[...].astype(F32) * own_live
    gx[16 : 16 + R, :] = own
    snd_g[...] = turned(own)
    rcopy(g_in.at[pl.ds(R - 16, 16)], gh.at[0], s_h.at[0], r_h.at[0], up).wait_recv()
    rcopy(g_in.at[pl.ds(0, 16)], gh.at[1], s_h.at[1], r_h.at[1], down).wait_recv()
    gx[0:16, :] = jnp.where(live_rows(me * R - 16, 16) > 0, gh[0].astype(F32), 0.0)
    gx[16 + R : 32 + R, :] = jnp.where(live_rows(me * R + R, 16) > 0, gh[1].astype(F32), 0.0)

    def grad_block(b, carry):
        at = cols(b)
        total = gx[16 : 16 + R, at]
        for t in range(T):
            total = total + ck_in[t : t + 1, at] * gx[pl.ds(16 + HALF - t, R), at]
        gx2 = (total * own_live).T.astype(BF16)
        for h in range(R // D):
            snd_d[(R // D) * b + h] = gx2[h * D : (h + 1) * D]
        return carry

    lax.fori_loop(0, Z * D // R, grad_block, 0)
    for i in zorder:
        p = (z + i) % Z
        send(rcopy(snd_d.at[p], dot_t.at[:, cols(z)], s_d.at[i], r_d.at[z], zpeer(p)))
    for i in zorder:
        p = (z + i) % Z
        send(rcopy(snd_g.at[p], gbuf.at[z], s_g.at[i], r_g.at[z], zpeer(p)))
    dot_t[:, cols(z)] = snd_d[z]
    gbuf[z] = snd_g[z]

    def halo(seq, n):
        mine = seq.at[pl.ds(c, Z), 1 - c]
        rcopy(mine, mine, s_h.at[n], r_h.at[n], gpeer(gm + 1 - 2 * c)).start()

        @pl.when(x != c)
        def _():
            rcopy(
                seq.at[c * Z, 1 - c], seq.at[(1 - c) * Z, 1 - c],
                s_h.at[n + 1], r_h.at[n + 1], gpeer(3 - gm),
            ).start()

    def halo_wait(seq, n):
        mine = seq.at[pl.ds(c, Z), 1 - c]
        other = seq.at[pl.ds(1 - c, Z), c]
        cp = rcopy(mine, other, s_h.at[n], r_h.at[n], gpeer(gm + 1 - 2 * c))
        cp.wait_send()
        cp.wait_recv()

        @pl.when(x != c)
        def _():
            cp2 = rcopy(
                seq.at[c * Z, 1 - c], seq.at[c * Z, c],
                s_h.at[n + 1], r_h.at[n + 1], gpeer(3 - gm),
            )
            cp2.wait_send()
            cp2.wait_recv()

    lane = lax.broadcasted_iota(jnp.int32, (1, R), 1)

    def live_of(j):
        return ((x * 2 * Z + 2 * j + c) * R + lane < length).astype(F32)

    def window(seq, j):
        p = 1 + 2 * j + c
        parts = [seq[(p + d) // 2, (p + d) % 2].astype(F32) for d in (-1, 0, 1)]
        return parts

    def arrive(n):
        rcopy(kv_at(n, gm), kv_at(n, gm), s_kv.at[0], r_kv.at[n], gpeer(across)).wait_recv()
        share(n)

    arrive(1)
    relay(0)
    if Z > 2:
        arrive(2)
    for i in zorder:
        p = (z + i) % Z
        rcopy(snd_q.at[p], qt.at[:, cols(p)], s_q.at[i], r_q.at[p], zpeer(p)).wait_recv()
    qaug[0:D, :] = (qt[...].astype(F32) * (D ** -0.5)).astype(BF16)

    lane_full = lax.broadcasted_iota(jnp.int32, (R, R), 1)
    sub_full = lax.broadcasted_iota(jnp.int32, (R, R), 0)

    def keys_at(n):
        return pl.ds(pl.multiple_of(n * CK, CK), CK)

    ones = jnp.ones((16, CK), BF16)

    def forward(n, carry):
        @pl.when(n < Z)
        def _():
            arrive(n)

        @pl.when(n - 2 < Z)
        def _():
            relay(n - 2)

        m = n - 3
        zs = (z + off_of(m)) % Z
        grp_copy(m, sib, 0, sib).wait_recv()
        grp_copy(m, across_sib, 2, sib).wait_recv()
        for g in range(4):
            blk = kvt[m, :, :, g * R : (g + 1) * R].reshape(2 * D, R).astype(F32).T
            at = pl.ds(pl.multiple_of(m * CK + g * R, R), R)
            kvn[at, :] = blk.astype(BF16)
            frame = ((g // 2) * 2 * Z + 2 * zs + g % 2) * R + sub_full
            fill = jnp.where((lane_full == D) & (frame >= length), FILL, 0.0)
            kaug[at, :] = jnp.where(lane_full < D, blk, fill).astype(BF16)
        at = keys_at(m)
        s = dot(kaug[at, :], qaug[...])
        m_old = m_run[0:1, :]
        m_new = jnp.maximum(m_old, jnp.max(s, axis=0, keepdims=True))
        w = jnp.exp(s - m_new)
        alpha = jnp.exp(m_old - m_new)
        wb = w.astype(BF16)
        w_all[at, :] = wb
        acc[...] = acc[...] * alpha + dot(jnp.concatenate([kvt[m, 1], ones], axis=0), wb)
        m_run[0:1, :] = m_new
        m_all[m, 0:1, :] = m_new
        return carry

    lax.fori_loop(3, Z + 3, forward, 0)

    for i in zorder:
        p = (z + i) % Z
        rcopy(snd_d.at[p], dot_t.at[:, cols(p)], s_d.at[i], r_d.at[p], zpeer(p)).wait_recv()


    inv = 1.0 / acc[D : D + 1, :]
    l_run[0:1, :] = inv
    att = (acc[0:D, :] * inv).astype(BF16)
    for j in range(Z):
        blk = (att[:, j * R : (j + 1) * R].astype(F32) * live_of(j)).astype(BF16)
        oseq[(1 + 2 * j + c) // 2, (1 + 2 * j + c) % 2] = blk
    halo(oseq, 2)
    m_run[1:2, :] = jnp.sum(dot_t[...].astype(F32) * att.astype(F32), axis=0, keepdims=True)

    HZ = Z // 2

    def out_block(j, carry):
        low, high = window(oseq, j), window(oseq, j + HZ)
        for n in range(3):
            ox[n * R : (n + 1) * R, :] = jnp.concatenate([low[n], high[n]], axis=0).T
        grad = jnp.concatenate([gbuf[j].astype(F32), gbuf[j + HZ].astype(F32)], axis=0).T
        total = ox[R : 2 * R, :]
        for t in range(T):
            seg = ox[pl.ds(R + t - HALF, R), :]
            total = total + kb[t : t + 1, :] * seg
            kga[t] = kga[t] + jnp.sum((grad * seg).reshape(R // 8, 8, R), axis=0)
        mixed = total.T
        mix_s[j] = (mixed[0:D] * live_of(j)).astype(BF16)
        mix_s[j + HZ] = (mixed[D : 2 * D] * live_of(j + HZ)).astype(BF16)
        return carry

    def mix_copy(i, p, h):
        return rcopy(mix_s.at[p], land.at[h, 0], s_m.at[i], r_m.at[h], zpeer(p))

    def taps_a(i):
        g = (gm + i) % 4
        return rcopy(kg_grp.at[gm], kg_grp.at[gm], s_kg.at[i], r_kg.at[gm], gpeer(g))

    def taps_a_in(i):
        g = (gm + i) % 4
        return rcopy(kg_grp.at[g], kg_grp.at[g], s_kg.at[i], r_kg.at[g], gpeer(g))

    def taps_b(i):
        return rcopy(kg_dp.at[dp], kg_dp.at[dp], s_kg.at[4 + i], r_kg.at[4 + dp], ((dp + i) % NDP, me))

    def taps_b_in(i):
        p = (dp + i) % NDP
        return rcopy(kg_dp.at[p], kg_dp.at[p], s_kg.at[4 + i], r_kg.at[4 + p], (p, me))

    def taps_c(i, p, h):
        return rcopy(kg_s, kg_land.at[h], s_kg.at[4 + NDP + i], r_kg.at[4 + NDP + h], zpeer(p))

    def part_copy(n, i):
        g = (gm + i) % 4
        return rcopy(part.at[n, :, :, cols(g)], gred.at[n, gm], s_p.at[n, i], r_p.at[n, gm], gpeer(g))

    def part_in(n, i):
        g = (gm + i) % 4
        return rcopy(part.at[n, :, :, cols(g)], gred.at[n, g], s_p.at[n, i], r_p.at[n, g], gpeer(g))

    def add_up(n):
        for i in range(1, 4):
            part_in(n, i).wait_recv()
        gred[n, gm] = part[n, :, :, cols(gm)]
        total = (gred[n, 0].astype(F32) + gred[n, 1].astype(F32)) + (
            gred[n, 2].astype(F32) + gred[n, 3].astype(F32)
        )
        kv_s[n] = total.astype(BF16)

    def kv_copy(n, h):
        return rcopy(kv_s.at[n], land.at[h, pl.ds(2, 2)], s_o.at[n], r_o.at[h], zpeer((z + off_of(n)) % Z))

    def dq_copy(i, p, h):
        return rcopy(dq_s.at[p], land.at[h, 1], s_dq.at[i], r_dq.at[h], zpeer(p))

    def backward(k, carry):
        n = Z - 1 - k
        at = keys_at(n)
        f = jnp.exp(m_all[n, 0:1, :] - m_run[0:1, :]) * l_run[0:1, :]
        gf = (dot_t[...].astype(F32) * f).astype(BF16)
        gfc[D : 2 * D, :] = gf
        dp_t = dot(kvn[at, :], gfc[...])
        wb = w_all[at, :]
        ds = (wb.astype(F32) * (dp_t - m_run[1:2, :] * f)).astype(BF16)
        dq_acc[...] = dq_acc[...] + dot(kvt[n, 0], ds)

        @pl.when(k == Z - 1)
        def _():
            for j in range(Z):
                dq_s[j] = (dq_acc[:, j * R : (j + 1) * R] * (D ** -0.5)).astype(BF16)
            for i in zorder:
                dq_copy(i, (z + i) % Z, z).start()

        part[n, 0] = (dot(qt[...], ds, NT) * (D ** -0.5)).astype(BF16)
        part[n, 1] = dot(gf, wb, NT).astype(BF16)
        for i in range(1, 4):
            part_copy(n, i).start()

        @pl.when(k > 1)
        def _():
            add_up(n + 2)
            kv_copy(n + 2, z).start()

        @pl.when(k == 0)
        def _():
            for i in zorder:
                p = (z + i) % Z
                rcopy(snd_g.at[p], gbuf.at[p], s_g.at[i], r_g.at[p], zpeer(p)).wait_recv()
            halo_wait(oseq, 2)
            lax.fori_loop(0, HZ, out_block, 0)
            for i in zorder:
                mix_copy(i, (z + i) % Z, z).start()
            kgt[...] = jnp.zeros_like(kgt)
            for t in range(T):
                kgt[t : t + 1, :] = jnp.sum(kga[t], axis=0, keepdims=True)
            rows = kgt[...]
            rows = rows + pltpu.roll(rows, D, 1)
            low_half = lax.broadcasted_iota(jnp.int32, (16, R), 1) < D
            kg_grp[gm] = jnp.where(low_half, rows[0:16], rows[16:32])
            for i in range(1, 4):
                taps_a(i).start()

        @pl.when(k == min(2, Z - 1))
        def _():
            for i in range(1, 4):
                taps_a_in(i).wait_recv()
            kg_dp[dp] = (kg_grp[0] + kg_grp[1]) + (kg_grp[2] + kg_grp[3])
            for i in range(1, NDP):
                taps_b(i).start()

        @pl.when(k == Z - 1)
        def _():
            for i in range(1, NDP):
                taps_b_in(i).wait_recv()
            total = kg_dp[0]
            for i in range(1, NDP):
                total = total + kg_dp[i]
            kg_s[...] = total.astype(BF16)
            for i in zorder:
                taps_c(i, (z + i) % Z, z).start()

        return carry

    lax.fori_loop(0, Z, backward, 0)


    add_up(1)
    kv_copy(1, z).start()
    add_up(0)
    local = [
        pltpu.make_async_copy(mix_s.at[z], land.at[z, 0], s_loc.at[0]),
        pltpu.make_async_copy(dq_s.at[z], land.at[z, 1], s_loc.at[1]),
        pltpu.make_async_copy(kv_s.at[0], land.at[z, pl.ds(2, 2)], s_loc.at[2]),
        pltpu.make_async_copy(kg_s, kg_land.at[z], s_loc.at[3]),
    ]
    for cp in local:
        cp.start()

    for cp in sends:
        cp.wait_send()

    def drain(n, carry):
        grp_copy(n, gm, 0, sib).wait_send()
        grp_copy(n, gm, 1, across).wait_send()
        grp_copy(n, across, 2, sib).wait_send()
        for i in range(1, 4):
            part_copy(n, i).wait_send()
        return carry

    lax.fori_loop(0, Z, drain, 0)
    for i in range(1, 4):
        taps_a(i).wait_send()
    for i in range(1, NDP):
        taps_b(i).wait_send()
    for i in zorder:
        p = (z + i) % Z
        for cp in (mix_copy(i, p, p), taps_c(i, p, p), dq_copy(i, p, p)):
            cp.wait_send()
            cp.wait_recv()
        kv_copy(slot_of[i], p).wait_send()
        kv_copy(slot_of[i], p).wait_recv()
    for cp in local:
        cp.wait()


def finish(Z, T, land, kg, mix_out, dq_out, dk_out, dv_out, kg_out):
    for n, out in enumerate((mix_out, dq_out, dk_out, dv_out)):
        out[...] = land[:, n].astype(F32).reshape(Z * D, R).T.astype(BF16)
    def taps_of(h):
        both = kg[h].astype(F32)
        return jnp.concatenate([both[:, 0:D], both[:, D : 2 * D]], axis=0)[0:T]

    for h in range(0, Z, 2):
        kg_out[:, h * D : (h + 2) * D] = jnp.concatenate([taps_of(h), taps_of(h + 1)], axis=1)


def per_device(Z, NDP, lengths, q, k, v, g, taps):
    W = Z * D
    NQ = R * Z
    NK = 4 * NQ
    T = taps.shape[0]
    CK = 4 * R
    vm = pltpu.VMEM
    dma = pltpu.SemaphoreType.DMA
    scratch = [
        vm((R, W), BF16), vm((R, W), BF16), vm((R, W), BF16), vm((R, W), BF16), vm((T, W), F32),
        vm((Z, 2, D, R), BF16), vm((Z, D, R), BF16), vm((Z, D, R), BF16), vm((Z, D, R), BF16),
        vm((R + 32, W), F32), vm((2, 16, W), BF16), vm((Z, D, R), BF16),
        vm((Z, 2, D, CK), BF16), vm((NK, 2 * D), BF16), vm((NK, 2 * D), BF16),
        vm((D, NQ), BF16), vm((2 * D, NQ), BF16),
        vm((Z + 1, 2, D, R), BF16),
        vm((D, NQ), BF16), vm((2 * D, NQ), BF16),
        vm((T, R), F32), vm((T, 8, R), F32), vm((32, R), F32), vm((3 * R, R), F32),
        vm((4, 16, R), F32), vm((NDP, 16, R), F32), vm((16, R), BF16),
        vm((NK, NQ), BF16), vm((Z, 8, NQ), F32), vm((8, NQ), F32), vm((8, NQ), F32),
        vm((D + 16, NQ), F32), vm((D, NQ), F32),
        vm((Z, D, R), BF16), vm((Z, D, R), BF16),
        vm((Z, 2, D, CK), BF16), vm((Z, 4, 2, D, R), BF16), vm((Z, 2, D, R), BF16),
        dma((5,)),
        dma((Z,)), dma((Z,)), dma((Z,)), dma((Z,)), dma((Z,)), dma((Z,)), dma((Z,)), dma((Z,)),
        dma((Z, 4)), dma((Z, 4)), dma((4,)), dma((4,)),
        dma((4 + NDP + Z,)), dma((4 + NDP + Z,)), dma((Z,)), dma((Z,)), dma((Z,)), dma((Z,)),
        dma((Z, 4)), dma((Z, 4)), dma((Z,)), dma((Z,)), dma((4,)),
    ]
    vspec = pl.BlockSpec(memory_space=pltpu.VMEM)
    anyspec = pl.BlockSpec(memory_space=pl.ANY)
    land, kg = pl.pallas_call(
        functools.partial(kernel, Z, NDP),
        out_shape=(
            jax.ShapeDtypeStruct((Z, 4, D, R), BF16),
            jax.ShapeDtypeStruct((Z, 16, R), BF16),
        ),
        in_specs=[pl.BlockSpec(memory_space=pltpu.SMEM)] + [anyspec] * 5,
        out_specs=(anyspec, anyspec),
        scratch_shapes=scratch,
        compiler_params=pltpu.CompilerParams(
            collective_id=0, has_side_effects=True, vmem_limit_bytes=56 * 1024 * 1024
        ),
        cost_estimate=pl.CostEstimate(
            flops=12 * NQ * NK * D, bytes_accessed=9 * R * W * 2, transcendentals=NQ * NK
        ),
    )(lengths, q[0], k[0], v[0], g[0], taps)
    outs = pl.pallas_call(
        functools.partial(finish, Z, T),
        out_shape=(
            jax.ShapeDtypeStruct((R, W), BF16), jax.ShapeDtypeStruct((R, W), BF16),
            jax.ShapeDtypeStruct((R, W), BF16), jax.ShapeDtypeStruct((R, W), BF16),
            jax.ShapeDtypeStruct((T, W), F32),
        ),
        in_specs=[vspec] * 2,
        out_specs=(vspec,) * 5,
    )(land, kg)
    return outs[0][None], outs[1][None], outs[2][None], outs[3][None], outs[4]


def solution(mesh):
    Z = mesh.shape["ctx"] // 4
    NDP = mesh.shape["dp"]
    split = P("dp", "ctx", None)
    return jax.shard_map(
        functools.partial(per_device, Z, NDP),
        mesh=mesh,
        in_specs=(P(), split, split, split, split, P()),
        out_specs=(split, split, split, split, P()),
        check_vma=False,
    )
```

```python
import functools

import jax
import jax.numpy as jnp
from jax import lax
from jax.experimental import pallas as pl
from jax.experimental.pallas import tpu as pltpu
from jax.sharding import PartitionSpec as P

MESH = pl.DeviceIdType.MESH
D = 64
R = 128
FILL = -1e30
F32 = jnp.float32
BF16 = jnp.bfloat16

NN = (((1,), (0,)), ((), ()))
NT = (((1,), (1,)), ((), ()))


def dot(a, b, dims=NN):
    return lax.dot_general(a, b, dims, preferred_element_type=F32)


def kernel(
    Z, NDP,
    len_ref, q_hbm, k_hbm, v_hbm, g_hbm, ck_hbm,
    land, kg_land,
    q_in, k_in, v_in, g_in, ck_in,
    snd_kv, snd_q, snd_g, snd_d, gx, gh, gbuf, kvt, kvn, kaug, qt, qaug, oseq, dot_t, gfc,
    kb, kga, kgt, ox, kg_grp, kg_dp, kg_s,
    w_all, m_all, m_run, l_run, acc, dq_acc, mix_s, dq_s, part, gred, kv_s,
    s_in, s_kv, r_kv, s_q, r_q, s_g, r_g, s_d, r_d, s_grp, r_grp, s_h, r_h,
    s_kg, r_kg, s_m, r_m, s_dq, r_dq, s_p, r_p, s_o, r_o, s_loc,
):
    NQ = R * Z
    CK = 4 * R
    T = ck_in.shape[0]
    HALF = (T - 1) // 2
    me = lax.axis_index("ctx")
    dp = lax.axis_index("dp")
    x = me // (2 * Z)
    z = (me // 2) % Z
    c = me % 2
    gm = 2 * x + c
    N = 4 * Z
    sib = gm + 1 - 2 * c
    across = (gm + 2) % 4
    across_sib = 3 - gm
    length = len_ref[dp]

    def zpeer(p):
        return (dp, x * 2 * Z + 2 * p + c)

    def gpeer(g):
        return (dp, (g // 2) * 2 * Z + 2 * z + g % 2)

    def rcopy(src, dst, ssem, rsem, dev):
        return pltpu.make_async_remote_copy(
            src_ref=src, dst_ref=dst, send_sem=ssem, recv_sem=rsem, device_id=dev, device_id_type=MESH
        )

    offs = [0]
    for i in range(1, Z // 2 + 1):
        offs.append(i)
        if Z - i != i:
            offs.append(Z - i)
    zorder = offs[1:]
    slot_of = {o: n for n, o in enumerate(offs)}

    def off_of(n):
        odd = n % 2
        return odd * ((n + 1) // 2) + (1 - odd) * ((Z - n // 2) % Z)

    zero_blk = jnp.zeros((D, R), BF16)
    oseq[0, 0] = zero_blk
    oseq[Z, 1] = zero_blk

    barrier = pltpu.get_barrier_semaphore()
    for i in range(1, Z):
        pl.semaphore_signal(barrier, inc=1, device_id=zpeer((z + i) % Z), device_id_type=MESH)
    for i in range(1, 4):
        pl.semaphore_signal(barrier, inc=1, device_id=gpeer((gm + i) % 4), device_id_type=MESH)
    for i in range(1, NDP):
        pl.semaphore_signal(barrier, inc=1, device_id=((dp + i) % NDP, me), device_id_type=MESH)
    pl.semaphore_signal(barrier, inc=1, device_id=(dp, (me + 2 * c - 1 + N) % N), device_id_type=MESH)

    loads = []
    for n, (a, b) in enumerate(((q_hbm, q_in), (k_hbm, k_in), (v_hbm, v_in), (g_hbm, g_in), (ck_hbm, ck_in))):
        cp = pltpu.make_async_copy(a, b, s_in.at[n])
        cp.start()
        loads.append(cp)

    turned = lambda a: a.astype(F32).T.astype(BF16).reshape(Z, D, R)
    loads[0].wait()
    snd_q[...] = turned(q_in[...])
    loads[1].wait()
    snd_kv[:, 0, :, :] = turned(k_in[...])
    loads[2].wait()
    snd_kv[:, 1, :, :] = turned(v_in[...])
    loads[3].wait()
    loads[4].wait()

    pl.semaphore_wait(barrier, (Z - 1) + 3 + (NDP - 1) + 1)

    def cols(j):
        return pl.ds(pl.multiple_of(j * R, R), R)

    def seq_at(ref, p):
        return ref.at[p // 2, p % 2]

    def kv_at(n, g):
        return kvt.at[n, :, :, cols(g)]

    sends = []

    def send(cp):
        cp.start()
        sends.append(cp)

    up, down = (dp, (me + 1) % N), (dp, (me + N - 1) % N)
    send(rcopy(g_in.at[pl.ds(R - 16, 16)], gh.at[0], s_h.at[0], r_h.at[0], up))
    send(rcopy(g_in.at[pl.ds(0, 16)], gh.at[1], s_h.at[1], r_h.at[1], down))

    def send_kv(near):
        for i in zorder:
            p = (z + i) % Z
            n = slot_of[Z - i]
            if (n < 3) == near:
                send(rcopy(snd_kv.at[p], kv_at(n, gm), s_kv.at[i], r_kv.at[n], zpeer(p)))

    send_kv(True)
    for i in zorder:
        p = (z + i) % Z
        send(rcopy(snd_q.at[p], qt.at[:, cols(z)], s_q.at[i], r_q.at[z], zpeer(p)))
    send_kv(False)
    kvt[0, :, :, cols(gm)] = snd_kv[z]

    def grp_copy(n, g, k, to):
        return rcopy(kv_at(n, g), kv_at(n, g), s_grp.at[n, k], r_grp.at[n, g], gpeer(to))

    def share(n):
        grp_copy(n, gm, 1, across).start()
        grp_copy(n, gm, 0, sib).start()

    def relay(n):
        grp_copy(n, across, 1, across).wait_recv()
        grp_copy(n, across, 2, sib).start()

    share(0)
    qt[:, cols(z)] = snd_q[z]

    pair = ck_in[:, cols(z // 2)]
    swapped = pltpu.roll(pair, D, 1)
    in_low = lax.broadcasted_iota(jnp.int32, (T, R), 1) // D
    kb[...] = jnp.where(in_low == z % 2, pair, swapped)
    kga[...] = jnp.zeros_like(kga)
    m_run[...] = jnp.full(m_run.shape, FILL, F32)
    l_run[...] = jnp.zeros_like(l_run)
    acc[...] = jnp.zeros_like(acc)
    dq_acc[...] = jnp.zeros_like(dq_acc)
    gfc[0:D, :] = jnp.zeros((D, NQ), BF16)
    row = lax.broadcasted_iota(jnp.int32, (D, NQ), 0)
    qaug[D : 2 * D, :] = jnp.where(row == 0, 1.0, 0.0).astype(BF16)

    def live_rows(first, count):
        frame = first + lax.broadcasted_iota(jnp.int32, (count, 1), 0)
        return ((frame >= 0) & (frame < length)).astype(F32)

    own_live = live_rows(me * R, R)
    own = g_in[...].astype(F32) * own_live
    gx[16 : 16 + R, :] = own
    snd_g[...] = turned(own)
    rcopy(g_in.at[pl.ds(R - 16, 16)], gh.at[0], s_h.at[0], r_h.at[0], up).wait_recv()
    rcopy(g_in.at[pl.ds(0, 16)], gh.at[1], s_h.at[1], r_h.at[1], down).wait_recv()
    gx[0:16, :] = jnp.where(live_rows(me * R - 16, 16) > 0, gh[0].astype(F32), 0.0)
    gx[16 + R : 32 + R, :] = jnp.where(live_rows(me * R + R, 16) > 0, gh[1].astype(F32), 0.0)

    def grad_block(b, carry):
        at = cols(b)
        total = gx[16 : 16 + R, at]
        for t in range(T):
            total = total + ck_in[t : t + 1, at] * gx[pl.ds(16 + HALF - t, R), at]
        gx2 = (total * own_live).T.astype(BF16)
        for h in range(R // D):
            snd_d[(R // D) * b + h] = gx2[h * D : (h + 1) * D]
        return carry

    lax.fori_loop(0, Z * D // R, grad_block, 0)
    for i in zorder:
        p = (z + i) % Z
        send(rcopy(snd_d.at[p], dot_t.at[:, cols(z)], s_d.at[i], r_d.at[z], zpeer(p)))
    for i in zorder:
        p = (z + i) % Z
        send(rcopy(snd_g.at[p], gbuf.at[z], s_g.at[i], r_g.at[z], zpeer(p)))
    dot_t[:, cols(z)] = snd_d[z]
    gbuf[z] = snd_g[z]

    def halo(seq, n):
        mine = seq.at[pl.ds(c, Z), 1 - c]
        rcopy(mine, mine, s_h.at[n], r_h.at[n], gpeer(gm + 1 - 2 * c)).start()

        @pl.when(x != c)
        def _():
            rcopy(
                seq.at[c * Z, 1 - c], seq.at[(1 - c) * Z, 1 - c],
                s_h.at[n + 1], r_h.at[n + 1], gpeer(3 - gm),
            ).start()

    def halo_wait(seq, n):
        mine = seq.at[pl.ds(c, Z), 1 - c]
        other = seq.at[pl.ds(1 - c, Z), c]
        cp = rcopy(mine, other, s_h.at[n], r_h.at[n], gpeer(gm + 1 - 2 * c))
        cp.wait_send()
        cp.wait_recv()

        @pl.when(x != c)
        def _():
            cp2 = rcopy(
                seq.at[c * Z, 1 - c], seq.at[c * Z, c],
                s_h.at[n + 1], r_h.at[n + 1], gpeer(3 - gm),
            )
            cp2.wait_send()
            cp2.wait_recv()

    lane = lax.broadcasted_iota(jnp.int32, (1, R), 1)

    def live_of(j):
        return ((x * 2 * Z + 2 * j + c) * R + lane < length).astype(F32)

    def window(seq, j):
        p = 1 + 2 * j + c
        parts = [seq[(p + d) // 2, (p + d) % 2].astype(F32) for d in (-1, 0, 1)]
        return parts

    def arrive(n):
        rcopy(kv_at(n, gm), kv_at(n, gm), s_kv.at[0], r_kv.at[n], gpeer(across)).wait_recv()
        share(n)

    arrive(1)
    relay(0)
    if Z > 2:
        arrive(2)
    for i in zorder:
        p = (z + i) % Z
        rcopy(snd_q.at[p], qt.at[:, cols(p)], s_q.at[i], r_q.at[p], zpeer(p)).wait_recv()
    qaug[0:D, :] = (qt[...].astype(F32) * (D ** -0.5)).astype(BF16)

    lane_full = lax.broadcasted_iota(jnp.int32, (R, R), 1)
    sub_full = lax.broadcasted_iota(jnp.int32, (R, R), 0)

    def keys_at(n):
        return pl.ds(pl.multiple_of(n * CK, CK), CK)

    ones = jnp.ones((16, CK), BF16)

    def forward(n, carry):
        @pl.when(n < Z)
        def _():
            arrive(n)

        @pl.when(n - 2 < Z)
        def _():
            relay(n - 2)

        m = n - 3
        zs = (z + off_of(m)) % Z
        grp_copy(m, sib, 0, sib).wait_recv()
        grp_copy(m, across_sib, 2, sib).wait_recv()
        for g in range(4):
            blk = kvt[m, :, :, g * R : (g + 1) * R].reshape(2 * D, R).astype(F32).T
            at = pl.ds(pl.multiple_of(m * CK + g * R, R), R)
            kvn[at, :] = blk.astype(BF16)
            frame = ((g // 2) * 2 * Z + 2 * zs + g % 2) * R + sub_full
            fill = jnp.where((lane_full == D) & (frame >= length), FILL, 0.0)
            kaug[at, :] = jnp.where(lane_full < D, blk, fill).astype(BF16)
        at = keys_at(m)
        s = dot(kaug[at, :], qaug[...])
        m_old = m_run[0:1, :]
        m_new = jnp.maximum(m_old, jnp.max(s, axis=0, keepdims=True))
        w = jnp.exp(s - m_new)
        alpha = jnp.exp(m_old - m_new)
        wb = w.astype(BF16)
        w_all[at, :] = wb
        acc[...] = acc[...] * alpha + dot(jnp.concatenate([kvt[m, 1], ones], axis=0), wb)
        m_run[0:1, :] = m_new
        m_all[m, 0:1, :] = m_new
        return carry

    lax.fori_loop(3, Z + 3, forward, 0)

    for i in zorder:
        p = (z + i) % Z
        rcopy(snd_d.at[p], dot_t.at[:, cols(p)], s_d.at[i], r_d.at[p], zpeer(p)).wait_recv()


    inv = 1.0 / acc[D : D + 1, :]
    l_run[0:1, :] = inv
    att = (acc[0:D, :] * inv).astype(BF16)
    for j in range(Z):
        blk = (att[:, j * R : (j + 1) * R].astype(F32) * live_of(j)).astype(BF16)
        oseq[(1 + 2 * j + c) // 2, (1 + 2 * j + c) % 2] = blk
    halo(oseq, 2)
    m_run[1:2, :] = jnp.sum(dot_t[...].astype(F32) * att.astype(F32), axis=0, keepdims=True)

    HZ = Z // 2

    def out_block(j, carry):
        low, high = window(oseq, j), window(oseq, j + HZ)
        for n in range(3):
            ox[n * R : (n + 1) * R, :] = jnp.concatenate([low[n], high[n]], axis=0).T
        grad = jnp.concatenate([gbuf[j].astype(F32), gbuf[j + HZ].astype(F32)], axis=0).T
        total = ox[R : 2 * R, :]
        for t in range(T):
            seg = ox[pl.ds(R + t - HALF, R), :]
            total = total + kb[t : t + 1, :] * seg
            kga[t] = kga[t] + jnp.sum((grad * seg).reshape(R // 8, 8, R), axis=0)
        mixed = total.T
        mix_s[j] = (mixed[0:D] * live_of(j)).astype(BF16)
        mix_s[j + HZ] = (mixed[D : 2 * D] * live_of(j + HZ)).astype(BF16)
        return carry

    def mix_copy(i, p, h):
        return rcopy(mix_s.at[p], land.at[h, 0], s_m.at[i], r_m.at[h], zpeer(p))

    def taps_a(i):
        g = (gm + i) % 4
        return rcopy(kg_grp.at[gm], kg_grp.at[gm], s_kg.at[i], r_kg.at[gm], gpeer(g))

    def taps_a_in(i):
        g = (gm + i) % 4
        return rcopy(kg_grp.at[g], kg_grp.at[g], s_kg.at[i], r_kg.at[g], gpeer(g))

    def taps_b(i):
        return rcopy(kg_dp.at[dp], kg_dp.at[dp], s_kg.at[4 + i], r_kg.at[4 + dp], ((dp + i) % NDP, me))

    def taps_b_in(i):
        p = (dp + i) % NDP
        return rcopy(kg_dp.at[p], kg_dp.at[p], s_kg.at[4 + i], r_kg.at[4 + p], (p, me))

    def taps_c(i, p, h):
        return rcopy(kg_s, kg_land.at[h], s_kg.at[4 + NDP + i], r_kg.at[4 + NDP + h], zpeer(p))

    def part_copy(n, i):
        g = (gm + i) % 4
        return rcopy(part.at[n, :, :, cols(g)], gred.at[n, gm], s_p.at[n, i], r_p.at[n, gm], gpeer(g))

    def part_in(n, i):
        g = (gm + i) % 4
        return rcopy(part.at[n, :, :, cols(g)], gred.at[n, g], s_p.at[n, i], r_p.at[n, g], gpeer(g))

    def add_up(n):
        for i in range(1, 4):
            part_in(n, i).wait_recv()
        gred[n, gm] = part[n, :, :, cols(gm)]
        total = (gred[n, 0].astype(F32) + gred[n, 1].astype(F32)) + (
            gred[n, 2].astype(F32) + gred[n, 3].astype(F32)
        )
        kv_s[n] = total.astype(BF16)

    def kv_copy(n, h):
        return rcopy(kv_s.at[n], land.at[h, pl.ds(2, 2)], s_o.at[n], r_o.at[h], zpeer((z + off_of(n)) % Z))

    def dq_copy(i, p, h):
        return rcopy(dq_s.at[p], land.at[h, 1], s_dq.at[i], r_dq.at[h], zpeer(p))

    def backward(k, carry):
        n = Z - 1 - k
        at = keys_at(n)
        f = jnp.exp(m_all[n, 0:1, :] - m_run[0:1, :]) * l_run[0:1, :]
        gf = (dot_t[...].astype(F32) * f).astype(BF16)
        gfc[D : 2 * D, :] = gf
        dp_t = dot(kvn[at, :], gfc[...])
        wb = w_all[at, :]
        ds = (wb.astype(F32) * (dp_t - m_run[1:2, :] * f)).astype(BF16)
        dq_acc[...] = dq_acc[...] + dot(kvt[n, 0], ds)

        @pl.when(k == Z - 1)
        def _():
            for j in range(Z):
                dq_s[j] = (dq_acc[:, j * R : (j + 1) * R] * (D ** -0.5)).astype(BF16)
            for i in zorder:
                dq_copy(i, (z + i) % Z, z).start()

        part[n, 0] = (dot(qt[...], ds, NT) * (D ** -0.5)).astype(BF16)
        part[n, 1] = dot(gf, wb, NT).astype(BF16)
        for i in range(1, 4):
            part_copy(n, i).start()

        @pl.when(k > 1)
        def _():
            add_up(n + 2)
            kv_copy(n + 2, z).start()

        @pl.when(k == 1)
        def _():
            for i in zorder:
                p = (z + i) % Z
                rcopy(snd_g.at[p], gbuf.at[p], s_g.at[i], r_g.at[p], zpeer(p)).wait_recv()
            halo_wait(oseq, 2)
            lax.fori_loop(0, HZ, out_block, 0)
            for i in zorder:
                mix_copy(i, (z + i) % Z, z).start()
            kgt[...] = jnp.zeros_like(kgt)
            for t in range(T):
                kgt[t : t + 1, :] = jnp.sum(kga[t], axis=0, keepdims=True)
            rows = kgt[...]
            rows = rows + pltpu.roll(rows, D, 1)
            low_half = lax.broadcasted_iota(jnp.int32, (16, R), 1) < D
            kg_grp[gm] = jnp.where(low_half, rows[0:16], rows[16:32])
            for i in range(1, 4):
                taps_a(i).start()

        @pl.when(k == min(3, Z - 1))
        def _():
            for i in range(1, 4):
                taps_a_in(i).wait_recv()
            kg_dp[dp] = (kg_grp[0] + kg_grp[1]) + (kg_grp[2] + kg_grp[3])
            for i in range(1, NDP):
                taps_b(i).start()

        @pl.when(k == Z - 1)
        def _():
            for i in range(1, NDP):
                taps_b_in(i).wait_recv()
            total = kg_dp[0]
            for i in range(1, NDP):
                total = total + kg_dp[i]
            kg_s[...] = total.astype(BF16)
            for i in zorder:
                taps_c(i, (z + i) % Z, z).start()

        return carry

    lax.fori_loop(0, Z, backward, 0)


    add_up(1)
    kv_copy(1, z).start()
    add_up(0)
    local = [
        pltpu.make_async_copy(mix_s.at[z], land.at[z, 0], s_loc.at[0]),
        pltpu.make_async_copy(dq_s.at[z], land.at[z, 1], s_loc.at[1]),
        pltpu.make_async_copy(kv_s.at[0], land.at[z, pl.ds(2, 2)], s_loc.at[2]),
        pltpu.make_async_copy(kg_s, kg_land.at[z], s_loc.at[3]),
    ]
    for cp in local:
        cp.start()

    for cp in sends:
        cp.wait_send()

    def drain(n, carry):
        grp_copy(n, gm, 0, sib).wait_send()
        grp_copy(n, gm, 1, across).wait_send()
        grp_copy(n, across, 2, sib).wait_send()
        for i in range(1, 4):
            part_copy(n, i).wait_send()
        return carry

    lax.fori_loop(0, Z, drain, 0)
    for i in range(1, 4):
        taps_a(i).wait_send()
    for i in range(1, NDP):
        taps_b(i).wait_send()
    for i in zorder:
        p = (z + i) % Z
        for cp in (mix_copy(i, p, p), taps_c(i, p, p), dq_copy(i, p, p)):
            cp.wait_send()
            cp.wait_recv()
        kv_copy(slot_of[i], p).wait_send()
        kv_copy(slot_of[i], p).wait_recv()
    for cp in local:
        cp.wait()


def finish(Z, T, land, kg, mix_out, dq_out, dk_out, dv_out, kg_out):
    for n, out in enumerate((mix_out, dq_out, dk_out, dv_out)):
        out[...] = land[:, n].astype(F32).reshape(Z * D, R).T.astype(BF16)
    def taps_of(h):
        both = kg[h].astype(F32)
        return jnp.concatenate([both[:, 0:D], both[:, D : 2 * D]], axis=0)[0:T]

    for h in range(0, Z, 2):
        kg_out[:, h * D : (h + 2) * D] = jnp.concatenate([taps_of(h), taps_of(h + 1)], axis=1)


def per_device(Z, NDP, lengths, q, k, v, g, taps):
    W = Z * D
    NQ = R * Z
    NK = 4 * NQ
    T = taps.shape[0]
    CK = 4 * R
    vm = pltpu.VMEM
    dma = pltpu.SemaphoreType.DMA
    scratch = [
        vm((R, W), BF16), vm((R, W), BF16), vm((R, W), BF16), vm((R, W), BF16), vm((T, W), F32),
        vm((Z, 2, D, R), BF16), vm((Z, D, R), BF16), vm((Z, D, R), BF16), vm((Z, D, R), BF16),
        vm((R + 32, W), F32), vm((2, 16, W), BF16), vm((Z, D, R), BF16),
        vm((Z, 2, D, CK), BF16), vm((NK, 2 * D), BF16), vm((NK, 2 * D), BF16),
        vm((D, NQ), BF16), vm((2 * D, NQ), BF16),
        vm((Z + 1, 2, D, R), BF16),
        vm((D, NQ), BF16), vm((2 * D, NQ), BF16),
        vm((T, R), F32), vm((T, 8, R), F32), vm((32, R), F32), vm((3 * R, R), F32),
        vm((4, 16, R), F32), vm((NDP, 16, R), F32), vm((16, R), BF16),
        vm((NK, NQ), BF16), vm((Z, 8, NQ), F32), vm((8, NQ), F32), vm((8, NQ), F32),
        vm((D + 16, NQ), F32), vm((D, NQ), F32),
        vm((Z, D, R), BF16), vm((Z, D, R), BF16),
        vm((Z, 2, D, CK), BF16), vm((Z, 4, 2, D, R), BF16), vm((Z, 2, D, R), BF16),
        dma((5,)),
        dma((Z,)), dma((Z,)), dma((Z,)), dma((Z,)), dma((Z,)), dma((Z,)), dma((Z,)), dma((Z,)),
        dma((Z, 4)), dma((Z, 4)), dma((4,)), dma((4,)),
        dma((4 + NDP + Z,)), dma((4 + NDP + Z,)), dma((Z,)), dma((Z,)), dma((Z,)), dma((Z,)),
        dma((Z, 4)), dma((Z, 4)), dma((Z,)), dma((Z,)), dma((4,)),
    ]
    vspec = pl.BlockSpec(memory_space=pltpu.VMEM)
    anyspec = pl.BlockSpec(memory_space=pl.ANY)
    land, kg = pl.pallas_call(
        functools.partial(kernel, Z, NDP),
        out_shape=(
            jax.ShapeDtypeStruct((Z, 4, D, R), BF16),
            jax.ShapeDtypeStruct((Z, 16, R), BF16),
        ),
        in_specs=[pl.BlockSpec(memory_space=pltpu.SMEM)] + [anyspec] * 5,
        out_specs=(anyspec, anyspec),
        scratch_shapes=scratch,
        compiler_params=pltpu.CompilerParams(
            collective_id=0, has_side_effects=True, vmem_limit_bytes=56 * 1024 * 1024
        ),
        cost_estimate=pl.CostEstimate(
            flops=12 * NQ * NK * D, bytes_accessed=9 * R * W * 2, transcendentals=NQ * NK
        ),
    )(lengths, q[0], k[0], v[0], g[0], taps)
    outs = pl.pallas_call(
        functools.partial(finish, Z, T),
        out_shape=(
            jax.ShapeDtypeStruct((R, W), BF16), jax.ShapeDtypeStruct((R, W), BF16),
            jax.ShapeDtypeStruct((R, W), BF16), jax.ShapeDtypeStruct((R, W), BF16),
            jax.ShapeDtypeStruct((T, W), F32),
        ),
        in_specs=[vspec] * 2,
        out_specs=(vspec,) * 5,
    )(land, kg)
    return outs[0][None], outs[1][None], outs[2][None], outs[3][None], outs[4]


def solution(mesh):
    Z = mesh.shape["ctx"] // 4
    NDP = mesh.shape["dp"]
    split = P("dp", "ctx", None)
    return jax.shard_map(
        functools.partial(per_device, Z, NDP),
        mesh=mesh,
        in_specs=(P(), split, split, split, split, P()),
        out_specs=(split, split, split, split, P()),
        check_vma=False,
    )
```
